32 devices in a mesh: ka: 2 (over y), sy: 4 (over x, core), sz: 4 (over z).
Axes of the slice: x: 2, y: 2, z: 4, core: 2. Of those that a mesh axis runs over, the one named last changes fastest.
Arguments:
- orbitals: bfloat16 [4, 4, 2, 32, 128, 128], P('ka', None, None, 'sy', 'sz'), may hold values from -7.5 to 7.5
- coefficients: float32 [4, 4], replicated, may hold values from -4 to 4
- local_pot: float32 [32, 128, 128], P('sy', 'sz'), may hold values from 0 to 2
- perturb: float32 [32, 128, 128], P('sy', 'sz'), may hold values from -4 to 6
- q_index: int32 [1], replicated, may hold values from 0 to 255
Outputs:
- responses: bfloat16 [4, 4, 2, 32, 128, 128], P('ka', None, None, 'sy', 'sz')
- density: float32 [32, 128, 128], P('sy', 'sz', 'ka')
The draws below stay inside these ranges and needn't reach their ends.
All inputs are finite; a program needn't handle non-finite values.
Results may differ from the reference program's by a relative error of at most 0.0035.
Values may be sent and summed in bfloat16 or wider, within the bound.
No kernel may reach another device: no remote copies, remote signals or barrier semaphores. Data moves between devices by JAX's collectives and lax.ppermute only.
A program may use at most 64 MiB of HBM per device.

```python
import jax
import jax.numpy as jnp
from jax import lax

NX = 128
K_DEV = 2
BANDS = 4
ITERS = 3
KPTS = 4
NY = 32
NZ = 128
N_KA = 2


def draw_orbitals(key, part):
    shared_key = jax.random.fold_in(key, 11)
    own_key = jax.random.fold_in(key, 12)
    shared_shape = (1, BANDS, 2, NY, NZ, NX)
    own_shape = (KPTS, BANDS, 2, NY, NZ, NX)
    shared = jax.random.truncated_normal(shared_key, -5.0, 5.0, shared_shape, jnp.float32)
    own = jax.random.truncated_normal(own_key, -5.0, 5.0, own_shape, jnp.float32)
    return (0.70710678 * (shared + own)).astype(jnp.bfloat16)


def draw_perturb(key, part):
    noise_key = jax.random.fold_in(key, 21)
    row_ramp = jnp.arange(NY, dtype=jnp.float32)[:, None, None] / NY
    depth_ramp = jnp.arange(NZ, dtype=jnp.float32)[None, :, None] / NZ
    ramp = 0.5 * (row_ramp + depth_ramp)
    smooth = 0.25 + 1.5 * ramp
    noise = jax.random.truncated_normal(noise_key, -3.5, 3.5, (NY, NZ, NX), jnp.float32)
    return (smooth + noise).astype(jnp.float32)


def levels(key, shape, shards, low, top_value):
    gain, own = 1.0, jax.random.fold_in(key, 6)
    for axis_at, blocks in shards:
        heights = jnp.exp(jax.random.uniform(jax.random.fold_in(own, axis_at), (blocks,), jnp.float32, low / len(shards), top_value / len(shards)))
        gain = gain * jnp.repeat(heights, shape[axis_at] // blocks).reshape([-1 if axis == axis_at else 1 for axis in range(len(shape))])
    return gain


def gaussian(stream_key, extent, deviation, reach, kind=jnp.bfloat16):
    return jnp.clip(deviation * jax.random.normal(stream_key, extent, jnp.float32), -reach, reach).astype(kind)


def setup_inputs(seed: int = 0) -> dict:
    streams_of = jax.random.split(jax.random.key(seed), 6)
    orbitals = draw_orbitals(jax.random.fold_in(streams_of[5], 71), 0)
    coefficients = gaussian(streams_of[1], (KPTS, ITERS + 1), 1.0, 4.0, jnp.float32)
    local_pot = jnp.clip(2.0 * jax.random.uniform(streams_of[2], (NY, NZ, NX), jnp.float32) ** levels(streams_of[2], (NY, NZ, NX), ((0, 4), (1, 4)), -0.2, 0.2), 0.0, 2.0)
    perturb = draw_perturb(jax.random.fold_in(streams_of[5], 71), 0)
    q_index = jax.random.randint(streams_of[4], (1,), 0, 128 * N_KA).astype(jnp.int32)
    return {"orbitals": orbitals, "coefficients": coefficients, "local_pot": local_pot, "perturb": perturb, "q_index": q_index}


centre_weight = -7.5
near_weight = 4.0 / 3.0
far_weight = -1.0 / 12.0
norm_epsilon = 1e-6


def apply_scaled(values, local_pot):
    summed = centre_weight * values
    for offset, weight in ((1, near_weight), (2, far_weight)):
        for axis_number in (1, 2, 3):
            summed = summed + weight * (jnp.roll(values, offset, axis_number) + jnp.roll(values, -offset, axis_number))
    energy_applied = -0.5 * summed + local_pot * values
    return 0.2 * energy_applied - values


def expand(source, coeffs, local_pot):
    previous = source
    current = apply_scaled(source, local_pot)
    result = coeffs[0] * previous + coeffs[1] * current
    for order in range(2, ITERS + 1):
        following = 2.0 * apply_scaled(current, local_pot) - previous
        result = result + coeffs[order] * following
        previous = current
        current = following
    return result


def project(source, partner_set):
    flat_source = source.reshape((BANDS, 2, -1))
    flat_partner = partner_set.astype(jnp.float32).reshape((BANDS, 2, -1))
    source_re = flat_source[:, 0]
    source_im = flat_source[:, 1]
    partner_re = flat_partner[:, 0]
    partner_im = flat_partner[:, 1]
    highest = lax.Precision.HIGHEST
    intersection_re = jnp.einsum('bm,cm->bc', partner_re, source_re, precision=highest) + jnp.einsum('bm,cm->bc', partner_im, source_im, precision=highest)
    intersection_im = jnp.einsum('bm,cm->bc', partner_re, source_im, precision=highest) - jnp.einsum('bm,cm->bc', partner_im, source_re, precision=highest)
    norms = jnp.sum(partner_re * partner_re + partner_im * partner_im, axis=1)
    coef_re = intersection_re / (norms[:, None] + norm_epsilon)
    coef_im = intersection_im / (norms[:, None] + norm_epsilon)
    correct_re = jnp.einsum('bc,bm->cm', coef_re, partner_re, precision=highest) - jnp.einsum('bc,bm->cm', coef_im, partner_im, precision=highest)
    correct_im = jnp.einsum('bc,bm->cm', coef_im, partner_re, precision=highest) + jnp.einsum('bc,bm->cm', coef_re, partner_im, precision=highest)
    correction = jnp.stack([correct_re, correct_im], 1)
    return (flat_source - correction).reshape(source.shape)


def roll_groups(array, first_slot):
    grouped = array.reshape((N_KA, K_DEV) + array.shape[1:])
    doubled = jnp.concatenate([grouped, grouped], 0)
    moved = lax.dynamic_slice_in_dim(doubled, first_slot, N_KA, 0)
    return moved.reshape(array.shape)


def reference(orbitals, coefficients, local_pot, perturb, q_index):
    shift_count = (q_index[0].astype(jnp.int32) % N_KA).astype(jnp.int32)
    received = roll_groups(orbitals, ((N_KA - shift_count) % N_KA).astype(jnp.int32))

    def one_point(inputs):
        orbital_set, partner_set, coeffs = inputs
        source = perturb[None, None] * orbital_set.astype(jnp.float32)
        projected = project(source, partner_set)
        flat = projected.reshape((BANDS * 2, NY, NZ, NX))
        return expand(flat, coeffs, local_pot).astype(jnp.bfloat16).reshape(orbital_set.shape)

    answer = lax.map(one_point, (received, orbitals, coefficients))
    responses = roll_groups(answer, shift_count)

    def accumulate(carry, inputs):
        orbital_set, response_set = inputs
        term = jnp.sum(orbital_set.astype(jnp.float32) * response_set.astype(jnp.float32), axis=(0, 1))
        return carry + term, None

    zeros = jnp.zeros((NY, NZ, NX), jnp.float32)
    summed, unused = lax.scan(accumulate, zeros, (orbitals, responses))
    density = summed * (2.0 / KPTS)
    return responses, density
```

```python
import functools

import jax
import jax.numpy as jnp
from jax import lax
from jax.experimental import pallas as pl
from jax.experimental.pallas import tpu as pltpu
from jax.sharding import PartitionSpec as P

ITERS = 3
REACH = 2
WIDE = REACH * ITERS
INNER = WIDE - REACH
TILE = 8

centre_weight = -7.5
near_weight = 4.0 / 3.0
far_weight = -1.0 / 12.0
norm_epsilon = 1e-06

near_scale = 0.4 * -0.5 * near_weight
far_scale = 0.4 * -0.5 * far_weight

f32 = jnp.float32
bf16 = jnp.bfloat16

VMEM_LIMIT = 40 * 1024 * 1024


def params():
    return pltpu.CompilerParams(vmem_limit_bytes=VMEM_LIMIT)


def whole():
    return pl.BlockSpec(memory_space=pltpu.VMEM)


def in_smem():
    return pl.BlockSpec(memory_space=pltpu.SMEM)


def pack_kernel(extras, *refs):
    field_ref = refs[0]
    extra_refs = refs[1 : 1 + extras]
    up_ref, down_ref, deep_up_ref, deep_down_ref = refs[1 + extras :]
    fields, rows, depth, _ = field_ref.shape

    def put(target, read):
        up_ref[target] = read(rows - WIDE, WIDE).astype(bf16)
        down_ref[target] = read(0, WIDE).astype(bf16)
        for pair in range(rows // 2):
            first = read(2 * pair, 1)[0].astype(f32)
            second = read(2 * pair + 1, 1)[0].astype(f32)
            deep_up_ref[target, pair] = jnp.concatenate(
                [first[depth - TILE :], second[depth - TILE :]], 0
            ).astype(bf16)
            deep_down_ref[target, pair] = jnp.concatenate(
                [first[:TILE], second[:TILE]], 0
            ).astype(bf16)

    def one(field, carry):
        put(field, lambda start, count: field_ref[field, pl.ds(start, count)])
        return carry

    lax.fori_loop(0, fields, one, 0)
    for index, ref in enumerate(extra_refs):
        put(fields + index, lambda start, count: ref[pl.ds(start, count)])


def pack(fields, extras):
    count, rows, depth, lanes = fields.shape
    total = count + len(extras)
    slab = jax.ShapeDtypeStruct((total, WIDE, depth, lanes), bf16)
    deep = jax.ShapeDtypeStruct((total, rows // 2, 2 * TILE, lanes), bf16)
    return pl.pallas_call(
        functools.partial(pack_kernel, len(extras)),
        out_shape=(slab, slab, deep, deep),
        in_specs=[whole()] * (1 + len(extras)),
        out_specs=(whole(),) * 4,
        compiler_params=params(),
        cost_estimate=pl.CostEstimate(
            flops=0, transcendentals=0, bytes_accessed=4 * count * rows * depth * lanes
        ),
        name="pack_halos",
    )(fields, *extras)


def to_next(value, axis):
    size = lax.axis_size(axis)
    return lax.ppermute(value, axis, [(i, (i + 1) % size) for i in range(size)])


def to_previous(value, axis):
    size = lax.axis_size(axis)
    return lax.ppermute(value, axis, [((i + 1) % size, i) for i in range(size)])


def exchange(fields, extras=()):
    up, down, deep_up, deep_down = pack(fields, extras)
    below = to_next(deep_up, "sz")
    above = to_previous(deep_down, "sz")
    before = to_next(up, "sy")
    after = to_previous(down, "sy")
    first_half = (lax.broadcasted_iota(jnp.int32, below.shape, 2) % TILE) < TILE // 2
    corner = jnp.where(first_half, above, below)
    pairs = INNER // 2
    corner_before = to_next(corner[:, corner.shape[1] - pairs :], "sy")
    corner_after = to_previous(corner[:, :pairs], "sy")
    return before, after, below, above, corner_before, corner_after


def inner_kernel(same, slots, *refs):
    if same:
        field_ref, perturb_ref, out_ref = refs
        partner_refs = [field_ref.at[slot] for slot in range(slots)]
    else:
        field_ref, perturb_ref = refs[:2]
        partner_refs = refs[2 : 2 + slots]
        out_ref = refs[2 + slots]
    fields, rows, depth, lanes = field_ref.shape[1:]
    bands = fields // 2
    steps = depth // (2 * TILE)
    count = 2 * bands * bands + bands

    for slot in range(slots):
        partner_ref = partner_refs[slot]

        def step(index, totals):
            totals = list(totals)
            row = index // steps
            start = pl.multiple_of((index % steps) * 2 * TILE, 2 * TILE)
            cells = pl.ds(start, 2 * TILE)
            raw = [field_ref[slot, f, row, cells].astype(f32) for f in range(fields)]
            if same:
                other = raw
            else:
                other = [partner_ref[f, row, cells].astype(f32) for f in range(fields)]
            kick = perturb_ref[row, cells]
            for half in range(2):
                part = slice(half * TILE, (half + 1) * TILE)
                source = [kick[part] * value[part] for value in raw]
                partner = [value[part] for value in other]
                at = 0
                for b in range(bands):
                    for c in range(bands):
                        totals[at] += (
                            partner[2 * b] * source[2 * c] + partner[2 * b + 1] * source[2 * c + 1]
                        )
                        at += 1
                for b in range(bands):
                    for c in range(bands):
                        totals[at] += (
                            partner[2 * b] * source[2 * c + 1] - partner[2 * b + 1] * source[2 * c]
                        )
                        at += 1
                for b in range(bands):
                    totals[at] += (
                        partner[2 * b] * partner[2 * b] + partner[2 * b + 1] * partner[2 * b + 1]
                    )
                    at += 1
            return tuple(totals)

        zero = jnp.zeros((TILE, lanes), f32)
        totals = lax.fori_loop(0, rows * steps, step, (zero,) * count)
        lines = [jnp.sum(total, axis=0, keepdims=True) for total in totals]
        square = bands * bands
        norms = [lines[2 * square + b] for b in range(bands) for c in range(bands)]
        out_ref[slot] = jnp.concatenate(lines[: 2 * square] + norms, 0)


def inner_products(orbitals, perturb, partners):
    slots, fields, _, _, lanes = orbitals.shape
    bands = fields // 2
    same = partners is None
    operands = (orbitals, perturb) + (() if same else tuple(partners))
    local = pl.pallas_call(
        functools.partial(inner_kernel, same, slots),
        out_shape=jax.ShapeDtypeStruct((slots, 3 * bands * bands, lanes), f32),
        in_specs=[whole()] * len(operands),
        out_specs=whole(),
        compiler_params=params(),
        cost_estimate=pl.CostEstimate(
            flops=36 * orbitals.size, transcendentals=0, bytes_accessed=2 * orbitals.size
        ),
        name="inner_products",
    )(*operands)
    size = lax.axis_size("sy")
    total = local
    for step in range(1, size):
        total = total + lax.ppermute(local, "sy", [(i, (i + step) % size) for i in range(size)])
    size = lax.axis_size("sz")
    pieces = [total]
    for step in range(1, size):
        pieces.append(lax.ppermute(total, "sz", [(i, (i + step) % size) for i in range(size)]))
    return pieces


def chain_kernel(slot, same, scale, pieces, last_slot, refs_in, *refs):
    refs = list(refs)
    named = dict(zip(refs_in, refs[: len(refs_in)]))
    response_ref, density_ref = refs[len(refs_in) : len(refs_in) + 2]
    t0_ref, t1_ref, t2_ref, diagonal_ref, factor_ref = refs[len(refs_in) + 2 :]
    field_ref = named["field"]
    fields, rows, depth, lanes = field_ref.shape[1:]
    bands = fields // 2
    square = bands * bands
    own_row = WIDE
    own_cell = TILE
    zero_shift = named["control"][1]

    total = named["piece0"][slot]
    for index in range(1, pieces):
        total = total + named["piece%d" % index][slot]
    summed = jnp.sum(total, axis=1, keepdims=True)
    norms = summed[2 * square :] + norm_epsilon
    for part in range(2):
        factors = summed[part * square : (part + 1) * square] / norms
        for index in range(square):
            factor_ref[part * square + index] = jnp.broadcast_to(
                factors[index : index + 1], (TILE, lanes)
            )

    def project(kick, read, read_partner, write):
        shape = (2, TILE, lanes)
        kick = kick.astype(f32).reshape(shape)
        raw = [read(f).astype(f32).reshape(shape) for f in range(fields)]
        partner = raw if same else [read_partner(f).astype(f32).reshape(shape) for f in range(fields)]
        for c in range(bands):
            real = kick * raw[2 * c]
            imag = kick * raw[2 * c + 1]
            for b in range(bands):
                re = factor_ref[b * bands + c]
                im = factor_ref[square + b * bands + c]
                real = real - (re * partner[2 * b] - im * partner[2 * b + 1])
                imag = imag - (im * partner[2 * b] + re * partner[2 * b + 1])
            write(2 * c, real)
            write(2 * c + 1, imag)

    halves = depth // (2 * TILE)

    def rows_of(names, extra, count, first):
        source_ref, partner_ref, kick_ref = names

        def one(index, carry):
            row = index // halves
            start = pl.multiple_of((index % halves) * 2 * TILE, 2 * TILE)
            cells = pl.ds(start, 2 * TILE)
            target = pl.ds(pl.multiple_of(start + own_cell, TILE), 2 * TILE)

            def write(f, value):
                t0_ref[f, first + row, target] = value.reshape((2 * TILE, lanes))

            project(
                kick_ref(row, cells),
                lambda f: source_ref[f, row, cells],
                lambda f: partner_ref[f, row, cells],
                write,
            )
            return carry

        lax.fori_loop(0, count * halves, one, 0)

    partner = (lambda name: named[name]) if same else (lambda name: named["partner_" + name])
    field_block = field_ref.at[0]
    rows_of(
        (field_block, field_block if same else named["partner_field"],
         lambda row, cells: named["perturb"][row, cells]),
        None, rows, own_row,
    )
    for name, first in (("before", 0), ("after", own_row + rows)):
        rows_of(
            (named[name], partner(name),
             lambda row, cells, name=name: named["kick_" + name][fields, row, cells]),
            None, WIDE, first,
        )

    def pairs_of(name, count, first, starts):
        def one(pair, carry):
            def write(f, value):
                for line in range(2):
                    for start in starts:
                        t0_ref[f, first + 2 * pair + line, start : start + TILE] = value[line]

            project(
                named["kick_" + name][fields, pair],
                lambda f: named[name][f, pair],
                lambda f: partner(name)[f, pair],
                write,
            )
            return carry

        lax.fori_loop(0, count, one, 0)

    above_cell = own_cell + depth
    pairs_of("below", rows // 2, own_row, (0,))
    pairs_of("above", rows // 2, own_row, (above_cell,))
    pairs_of("corner_before", INNER // 2, own_row - INNER, (0, above_cell))
    pairs_of("corner_after", INNER // 2, own_row + rows, (0, above_cell))

    def diagonal(value):
        return 0.4 * (value.astype(f32) - 0.5 * centre_weight) - 2.0

    whole_depth = pl.ds(own_cell, depth)
    for row in range(rows):
        diagonal_ref[own_row + row, whole_depth] = diagonal(named["local_pot"][row])
    for row in range(INNER):
        diagonal_ref[own_row - INNER + row, whole_depth] = diagonal(
            named["kick_before"][fields + 1, WIDE - INNER + row]
        )
        diagonal_ref[own_row + rows + row, whole_depth] = diagonal(
            named["kick_after"][fields + 1, row]
        )

    def diagonal_pairs(name, count, first, starts):
        for pair in range(count):
            value = diagonal(named["kick_" + name][fields + 1, pair])
            for line in range(2):
                for start in starts:
                    diagonal_ref[first + 2 * pair + line, start : start + TILE] = value[
                        line * TILE : (line + 1) * TILE
                    ]

    diagonal_pairs("below", rows // 2, own_row, (0,))
    diagonal_pairs("above", rows // 2, own_row, (above_cell,))
    diagonal_pairs("corner_before", INNER // 2, own_row - INNER, (0, above_cell))
    diagonal_pairs("corner_after", INNER // 2, own_row + rows, (0, above_cell))

    row_index = named["control"][0]
    weights = [named["coefficients"][row_index, order] for order in range(ITERS + 1)]

    if slot == 0:
        density_ref[...] = jnp.zeros_like(density_ref)
    else:
        density_ref[...] = named["density"][...]

    half = TILE // 2
    moved = half
    middle = depth + 2 * half

    def twice(read, row, start, count, factor):
        centre = read(row, start, count)
        near = pltpu.roll(centre, 1, 1) + pltpu.roll(centre, lanes - 1, 1)
        far = pltpu.roll(centre, 2, 1) + pltpu.roll(centre, lanes - 2, 1)
        near = near + (read(row - 1, start, count) + read(row + 1, start, count))
        far = far + (read(row - 2, start, count) + read(row + 2, start, count))
        near = near + (read(row, start - 1, count) + read(row, start + 1, count))
        far = far + (read(row, start - 2, count) + read(row, start + 2, count))
        return centre, factor * centre + (near_scale * near + far_scale * far)

    def one_field(f, carry):
        def reader(ref, at_field, offset):
            def read(row, start, count):
                return ref[at_field, row, pl.ds(start + offset + zero_shift, count)]

            return read

        read0 = lambda row, start, count: t0_ref[f, row, pl.ds(start + zero_shift, count)]
        read1 = lambda row, start, count: t1_ref[row, pl.ds(start + moved + zero_shift, count)]
        read2 = lambda row, start, count: t2_ref[row, pl.ds(start + moved + zero_shift, count)]
        read_factor = lambda row, start, count: diagonal_ref[row, pl.ds(start + zero_shift, count)]

        def spans(outer, inner):
            for row in range(own_row - outer, own_row + rows + outer):
                if own_row - inner <= row < own_row + rows + inner:
                    yield row, own_cell - half, middle
                else:
                    yield row, own_cell, depth

        for row, start, count in spans(INNER, INNER - REACH):
            _, value = twice(read0, row, start, count, read_factor(row, start, count))
            t1_ref[row, pl.ds(start + moved, count)] = 0.5 * value
        for row, start, count in spans(REACH, 0):
            _, value = twice(read1, row, start, count, read_factor(row, start, count))
            t2_ref[row, pl.ds(start + moved, count)] = value - read0(row, start, count)
        for row in range(own_row, own_row + rows):
            second, value = twice(read2, row, own_cell, depth, read_factor(row, own_cell, depth))
            first = read1(row, own_cell, depth)
            third = value - first
            answer = (
                weights[0] * read0(row, own_cell, depth) + weights[1] * first
            ) + weights[2] * second
            answer = (answer + weights[3] * third).astype(bf16)
            response_ref[0, f, row - own_row] = answer
            density_ref[row - own_row] += answer.astype(f32) * field_ref[
                0, f, row - own_row
            ].astype(f32)
        return carry

    lax.fori_loop(0, fields, one_field, 0)
    if last_slot:
        density_ref[...] = density_ref[...] * scale


HALO_NAMES = ("before", "after", "below", "above", "corner_before", "corner_after")


def chain(slot, orbitals, partner, halo, kick_halo, partner_halo, perturb, local_pot, coefficients,
          control, pieces, scale, carried):
    slots, fields, rows, depth, lanes = orbitals.shape
    same = partner is None
    names, operands, specs = [], [], []

    def add(name, value, spec):
        names.append(name)
        operands.append(value)
        specs.append(spec)

    block = (1, fields, rows, depth, lanes)
    at_slot = pl.BlockSpec(block, lambda step: (slot, 0, 0, 0, 0))
    add("field", orbitals, at_slot)
    for name, value in zip(HALO_NAMES, halo):
        add(name, value, whole())
    if slot:
        for name, value in zip(HALO_NAMES, kick_halo):
            add("kick_" + name, value, whole())
    if not same:
        add("partner_field", partner, whole())
        for name, value in zip(HALO_NAMES, partner_halo):
            add("partner_" + name, value, whole())
    add("perturb", perturb, whole())
    add("local_pot", local_pot, whole())
    add("coefficients", coefficients, in_smem())
    add("control", control, in_smem())
    for index, value in enumerate(pieces):
        add("piece%d" % index, value, whole())
    aliases = {}
    if slot:
        add("density", carried[1], whole())
        aliases = {len(names): 0}
        add("response", carried[0], pl.BlockSpec(memory_space=pl.ANY))

    def kernel(*refs):
        alias = dict(zip(names, refs))
        full_names = list(names)
        refs = list(refs)
        inputs = refs[: len(names)]
        if not slot:
            for name in HALO_NAMES:
                full_names.append("kick_" + name)
                inputs.append(alias[name])
        chain_kernel(
            slot, same, scale, len(pieces), slot == slots - 1, full_names, *inputs, *refs[len(names) :]
        )

    long_rows = rows + 2 * WIDE
    long_depth = depth + 2 * TILE
    return pl.pallas_call(
        kernel,
        grid=(1,),
        out_shape=(
            jax.ShapeDtypeStruct(orbitals.shape, bf16),
            jax.ShapeDtypeStruct((rows, depth, lanes), f32),
        ),
        in_specs=specs,
        out_specs=(at_slot, whole()),
        scratch_shapes=[
            pltpu.VMEM((fields, long_rows, long_depth, lanes), f32),
            pltpu.VMEM((long_rows, long_depth + TILE, lanes), f32),
            pltpu.VMEM((long_rows, long_depth + TILE, lanes), f32),
            pltpu.VMEM((long_rows, long_depth, lanes), f32),
            pltpu.VMEM((fields * fields // 2, TILE, lanes), f32),
        ],
        input_output_aliases=aliases,
        compiler_params=params(),
        cost_estimate=pl.CostEstimate(
            flops=200 * fields * rows * depth * lanes,
            transcendentals=0,
            bytes_accessed=8 * fields * rows * depth * lanes,
        ),
        name="response_chain",
    )(*operands)


def from_behind(value, axis, steps):
    count = lax.axis_size(axis)
    pairs = [(source, (source + steps) % count) for source in range(count)]
    return lax.ppermute(value, axis, pairs)


def route(blocks, shift_count):
    groups = lax.axis_size("ka")
    if groups == 2:
        return from_behind(blocks, "ka", -1)
    moved = blocks
    for bit_index in range((groups - 1).bit_length()):
        shifted = from_behind(moved, "ka", -(1 << bit_index))
        taken = shift_count >> bit_index & 1 == 1
        moved = jnp.where(taken, shifted, moved)
    return moved


def combine(partial_sum):
    groups = lax.axis_size("ka")
    if groups != 2:
        return lax.psum_scatter(partial_sum, "ka", scatter_dimension=2, tiled=True)
    lanes = partial_sum.shape[2] // 2
    first = lax.axis_index("ka") == 0
    low, high = partial_sum[:, :, :lanes], partial_sum[:, :, lanes:]
    return jnp.where(first, low, high) + from_behind(jnp.where(first, high, low), "ka", 1)


def body(orbitals, coefficients, local_pot, perturb, q_index):
    groups = lax.axis_size("ka")
    shift_count = q_index[0] % groups
    group_index = lax.axis_index("ka")
    slots, bands, parts, rows, depth, lanes = orbitals.shape
    fields = orbitals.reshape((slots, bands * parts, rows, depth, lanes))
    partner_group = (group_index + shift_count) % groups
    scale = 2.0 / (slots * groups)

    def work(shifted):
        halos = [
            exchange(fields[slot], (perturb, local_pot) if slot == 0 else ()) for slot in range(slots)
        ]
        partners, partner_halos = [None] * slots, [None] * slots
        if shifted:
            partners = [route(fields[slot], shift_count) for slot in range(slots)]
            partner_halos = [exchange(partner) for partner in partners]
        pieces = inner_products(fields, perturb, partners if shifted else None)
        carried = None
        for slot in range(slots):
            row_index = partner_group * slots + slot
            control = jnp.stack([row_index, jnp.zeros_like(row_index)]).astype(jnp.int32)
            carried = chain(
                slot, fields, partners[slot], halos[slot], halos[0], partner_halos[slot],
                perturb, local_pot, coefficients, control, pieces, scale, carried,
            )
        return carried

    responses, partial_sum = lax.cond(
        shift_count == 0, lambda: work(False), lambda: work(True)
    )
    return responses.reshape(orbitals.shape), combine(partial_sum)


def solution(mesh):
    return jax.shard_map(
        body,
        mesh=mesh,
        in_specs=(
            P("ka", None, None, "sy", "sz", None),
            P(),
            P("sy", "sz", None),
            P("sy", "sz", None),
            P(),
        ),
        out_specs=(P("ka", None, None, "sy", "sz", None), P("sy", "sz", "ka")),
        check_vma=False,
    )
```

```python
import functools

import jax
import jax.numpy as jnp
from jax import lax
from jax.experimental import pallas as pl
from jax.experimental.pallas import tpu as pltpu
from jax.sharding import PartitionSpec as P

ITERS = 3
REACH = 2
WIDE = REACH * ITERS
INNER = WIDE - REACH
TILE = 8

centre_weight = -7.5
near_weight = 4.0 / 3.0
far_weight = -1.0 / 12.0
norm_epsilon = 1e-06

near_scale = 0.4 * -0.5 * near_weight
far_scale = 0.4 * -0.5 * far_weight

f32 = jnp.float32
bf16 = jnp.bfloat16

VMEM_LIMIT = 40 * 1024 * 1024
GROUP = 2
NO_COST = pl.CostEstimate(flops=0, transcendentals=0, bytes_accessed=0)


def params():
    return pltpu.CompilerParams(vmem_limit_bytes=VMEM_LIMIT)


def whole():
    return pl.BlockSpec(memory_space=pltpu.VMEM)


def in_smem():
    return pl.BlockSpec(memory_space=pltpu.SMEM)


def pack_kernel(slots, fields, extras, *refs):
    block_refs = refs[: 1 + extras]
    up_ref, down_ref, deep_up_ref, deep_down_ref = refs[1 + extras :]
    rows, depth = block_refs[0].shape[-3:-1]

    def put(read, slab_index, deep_index):
        if slab_index is not None:
            up_ref[slab_index] = read(rows - WIDE, WIDE).astype(bf16)
            down_ref[slab_index] = read(0, WIDE).astype(bf16)
        for pair in range(rows // 2):
            first = read(2 * pair, 1)[0].astype(f32)
            second = read(2 * pair + 1, 1)[0].astype(f32)
            deep_up_ref[deep_index, pair] = jnp.concatenate(
                [first[depth - TILE :], second[depth - TILE :]], 0
            ).astype(bf16)
            deep_down_ref[deep_index, pair] = jnp.concatenate(
                [first[:TILE], second[:TILE]], 0
            ).astype(bf16)

    for slot in range(slots):

        def one(field, carry, slot=slot):
            put(
                lambda start, count: block_refs[0][slot, field, pl.ds(start, count)],
                None if slot else field,
                slot * fields + field,
            )
            return carry

        lax.fori_loop(0, fields, one, 0)
    for index in range(extras):
        ref = block_refs[1 + index]
        put(
            lambda start, count, ref=ref: ref[pl.ds(start, count)],
            fields + index,
            slots * fields + index,
        )


def pack(blocks, extras):
    slots, fields, rows, depth, lanes = blocks.shape
    count = fields + len(extras)
    shapes = [jax.ShapeDtypeStruct((count, WIDE, depth, lanes), bf16)] * 2
    total = slots * fields + len(extras)
    shapes += [jax.ShapeDtypeStruct((total, rows // 2, 2 * TILE, lanes), bf16)] * 2
    return pl.pallas_call(
        functools.partial(pack_kernel, slots, fields, len(extras)),
        out_shape=tuple(shapes),
        in_specs=[whole()] * (1 + len(extras)),
        out_specs=(whole(),) * len(shapes),
        compiler_params=params(),
        cost_estimate=NO_COST,
        name="pack_halos",
    )(blocks, *extras)


def pack_rows_kernel(block_ref, *refs):
    up_ref, down_ref = refs[-2:]
    rows = block_ref.shape[2]
    up_ref[...] = block_ref[0, :, rows - WIDE :]
    down_ref[...] = block_ref[0, :, :WIDE]


def pack_rows(blocks, slot, after):
    _, fields, rows, depth, lanes = blocks.shape
    shape = jax.ShapeDtypeStruct((fields, WIDE, depth, lanes), bf16)
    block = pl.BlockSpec((1, fields, rows, depth, lanes), lambda step: (slot, 0, 0, 0, 0))
    return pl.pallas_call(
        pack_rows_kernel,
        grid=(1,),
        out_shape=(shape, shape),
        in_specs=[block] + [pl.BlockSpec(memory_space=pl.ANY)] * len(after),
        out_specs=(whole(), whole()),
        compiler_params=params(),
        cost_estimate=NO_COST,
        name="pack_rows",
    )(blocks, *after)


def to_next(value, axis):
    size = lax.axis_size(axis)
    return lax.ppermute(value, axis, [(i, (i + 1) % size) for i in range(size)])


def to_previous(value, axis):
    size = lax.axis_size(axis)
    return lax.ppermute(value, axis, [((i + 1) % size, i) for i in range(size)])


def exchange(blocks, extras=()):
    slots = blocks.shape[0]
    up, down, deep_up, deep_down = pack(blocks, extras)
    rows = [(to_next(up, "sy"), to_previous(down, "sy"))]
    for slot in range(1, slots):
        up, down = pack_rows(blocks, slot, rows[-1])
        rows.append((to_next(up, "sy"), to_previous(down, "sy")))
    below = to_next(deep_up, "sz")
    above = to_previous(deep_down, "sz")
    first_half = (lax.broadcasted_iota(jnp.int32, below.shape, 2) % TILE) < TILE // 2
    corner = jnp.where(first_half, above, below)
    pairs = INNER // 2
    corner_before = to_next(corner[:, corner.shape[1] - pairs :], "sy")
    corner_after = to_previous(corner[:, :pairs], "sy")
    return rows, (below, above, corner_before, corner_after)


def inner_kernel(same, slots, *refs):
    if same:
        field_ref, perturb_ref, out_ref = refs
        partner_refs = field_ref
    else:
        field_ref, partner_refs, perturb_ref, out_ref = refs
    fields, rows, depth, lanes = field_ref.shape[1:]
    bands = fields // 2
    steps = depth // (2 * TILE)
    count = 2 * bands * bands + bands

    for slot in range(slots):

        def step(index, totals, slot=slot):
            totals = list(totals)
            row = index // steps
            start = pl.multiple_of((index % steps) * 2 * TILE, 2 * TILE)
            cells = pl.ds(start, 2 * TILE)
            raw = [field_ref[slot, f, row, cells].astype(f32) for f in range(fields)]
            if same:
                other = raw
            else:
                other = [partner_refs[slot, f, row, cells].astype(f32) for f in range(fields)]
            kick = perturb_ref[row, cells]
            for half in range(2):
                part = slice(half * TILE, (half + 1) * TILE)
                source = [kick[part] * value[part] for value in raw]
                partner = [value[part] for value in other]
                at = 0
                for b in range(bands):
                    for c in range(bands):
                        totals[at] += (
                            partner[2 * b] * source[2 * c] + partner[2 * b + 1] * source[2 * c + 1]
                        )
                        at += 1
                for b in range(bands):
                    for c in range(bands):
                        totals[at] += (
                            partner[2 * b] * source[2 * c + 1] - partner[2 * b + 1] * source[2 * c]
                        )
                        at += 1
                for b in range(bands):
                    totals[at] += (
                        partner[2 * b] * partner[2 * b] + partner[2 * b + 1] * partner[2 * b + 1]
                    )
                    at += 1
            return tuple(totals)

        zero = jnp.zeros((TILE, lanes), f32)
        totals = lax.fori_loop(0, rows * steps, step, (zero,) * count)
        lines = [jnp.sum(total, axis=0, keepdims=True) for total in totals]
        square = bands * bands
        norms = [lines[2 * square + b] for b in range(bands) for c in range(bands)]
        out_ref[slot] = jnp.concatenate(lines[: 2 * square] + norms, 0)


def inner_products(orbitals, perturb, partners):
    slots, fields, _, _, lanes = orbitals.shape
    bands = fields // 2
    same = partners is None
    operands = (orbitals,) + (() if same else (partners,)) + (perturb,)
    local = pl.pallas_call(
        functools.partial(inner_kernel, same, slots),
        out_shape=jax.ShapeDtypeStruct((slots, 3 * bands * bands, lanes), f32),
        in_specs=[whole()] * len(operands),
        out_specs=whole(),
        compiler_params=params(),
        cost_estimate=NO_COST,
        name="inner_products",
    )(*operands)
    size = lax.axis_size("sy")
    total = local
    for step in range(1, size):
        total = total + lax.ppermute(local, "sy", [(i, (i + step) % size) for i in range(size)])
    size = lax.axis_size("sz")
    pieces = [total]
    for step in range(1, size):
        pieces.append(lax.ppermute(total, "sz", [(i, (i + step) % size) for i in range(size)]))
    return pieces


def factor_kernel(fields, depth, *refs):
    piece_refs, (high_ref, low_ref) = refs[:-2], refs[-2:]
    bands = fields // 2
    square = bands * bands
    size = fields * depth
    total = piece_refs[0][...]
    for ref in piece_refs[1:]:
        total = total + ref[...]
    lane = lax.broadcasted_iota(jnp.int32, (1, size), 1)
    cell = lax.broadcasted_iota(jnp.int32, (depth, size), 0)
    same_cell = lax.broadcasted_iota(jnp.int32, (depth, size), 1) % depth == cell
    for slot in range(total.shape[0]):
        summed = jnp.sum(total[slot], axis=1, keepdims=True)
        norms = summed[2 * square :] + norm_epsilon
        real = summed[:square] / norms
        imag = summed[square : 2 * square] / norms
        for out in range(fields):
            c, part = out // 2, out % 2
            line = jnp.zeros((1, size), f32)
            for b in range(bands):
                re = real[b * bands + c : b * bands + c + 1]
                im = imag[b * bands + c : b * bands + c + 1]
                first, second = (im, re) if part else (re, -im)
                line = jnp.where(lane // depth == 2 * b, first, line)
                line = jnp.where(lane // depth == 2 * b + 1, second, line)
            high = line.astype(bf16).astype(f32)
            for ref, value in ((high_ref, high), (low_ref, line - high)):
                spread = jnp.broadcast_to(value, (depth, size))
                ref[slot, pl.ds(out * depth, depth)] = jnp.where(same_cell, spread, 0.0).astype(bf16)


def factors(pieces, slots, fields, depth):
    shape = jax.ShapeDtypeStruct((slots, fields * depth, fields * depth), bf16)
    return pl.pallas_call(
        functools.partial(factor_kernel, fields, depth),
        out_shape=(shape, shape),
        in_specs=[whole()] * len(pieces),
        out_specs=(whole(), whole()),
        compiler_params=params(),
        cost_estimate=NO_COST,
        name="projection_factors",
    )(*pieces)


def chain_kernel(slot, same, scale, last_slot, split, named, response_ref, density_refs, scratch):
    t0_ref, t1_ref, t2_ref, diagonal_ref, sum_ref = scratch
    field_ref = named["field"]
    fields, rows, depth, lanes = field_ref.shape[1:]
    own_row = WIDE
    own_cell = TILE
    zero_shift = named["control"][1]
    high = named["high"][0]
    low = named["low"][0]
    size = fields * depth
    block = (fields, depth, lanes)

    def project(pieces):
        raws = [raw for raw, _, _, _ in pieces]
        others = raws if same else [partner for _, partner, _, _ in pieces]
        stacked = jnp.concatenate([other.reshape((size, lanes)) for other in others], 1)
        along = jnp.dot(high, stacked, preferred_element_type=f32)
        along = along + jnp.dot(low, stacked, preferred_element_type=f32)
        results = []
        for index, (raw, _, kick, _) in enumerate(pieces):
            part = along[:, index * lanes : (index + 1) * lanes].reshape(block)
            results.append(kick.astype(f32)[None] * raw.astype(f32) - part)
        for result, (_, _, _, write) in zip(results, pieces):
            write(result)

    partner_own = (lambda row: None) if same else (lambda row: named["partner_field"][0, :, row])
    partner_halo = (
        (lambda name, index: None) if same else (lambda name, index: named["partner_" + name][index])
    )
    depth_cells = pl.ds(own_cell, depth)

    def own(pair, carry):
        def piece(row):
            def write(value):
                t0_ref[:, own_row + row, depth_cells] = value

            return field_ref[0, :, row], partner_own(row), named["perturb"][row], write

        project([piece(2 * pair), piece(2 * pair + 1)])
        return carry

    lax.fori_loop(0, rows // 2, own, 0)

    def outer(row, carry):
        def piece(name, first):
            def write(value):
                t0_ref[:, first + row, depth_cells] = value

            index = (pl.ds(0, fields), row)
            kick = named["kick_" + name][fields, row]
            return named[name][index], partner_halo(name, index), kick, write

        project([piece("before", 0), piece("after", own_row + rows)])
        return carry

    lax.fori_loop(0, WIDE, outer, 0)

    pairs = depth // (2 * TILE)
    above_cell = own_cell + depth
    extra = named["below"].shape[0] - 2

    def deep(group, names, firsts, starts):
        def piece(name, first, starts):
            def write(value):
                for line in range(2 * pairs):
                    cells = value[:, line * TILE : (line + 1) * TILE]
                    for start in starts:
                        t0_ref[:, first + 2 * pairs * group + line, start : start + TILE] = cells

            index = (pl.ds(slot * fields, fields), pl.ds(group * pairs, pairs))
            partner = partner_halo(name, index)
            if partner is not None:
                partner = partner.reshape(block)
            kick = named[name][extra, pl.ds(group * pairs, pairs)].reshape((depth, lanes))
            return named[name][index].reshape(block), partner, kick, write

        project([piece(*each) for each in zip(names, firsts, starts)])

    def deep_own(group, carry):
        deep(group, ("below", "above"), (own_row, own_row), ((0,), (above_cell,)))
        return carry

    lax.fori_loop(0, rows // (2 * pairs), deep_own, 0)
    for group in range(INNER // (2 * pairs)):
        both = (0, above_cell)
        firsts = (own_row - INNER, own_row + rows)
        deep(group, ("corner_before", "corner_after"), firsts, (both, both))

    half = TILE // 2
    moved = half
    middle = depth + 2 * half

    def diagonal(value):
        return 0.4 * (value.astype(f32) - 0.5 * centre_weight) - 2.0

    for row in range(rows):
        diagonal_ref[own_row + row, depth_cells] = diagonal(named["local_pot"][row])
    for row in range(INNER):
        diagonal_ref[own_row - INNER + row, depth_cells] = diagonal(
            named["kick_before"][fields + 1, WIDE - INNER + row]
        )
        diagonal_ref[own_row + rows + row, depth_cells] = diagonal(
            named["kick_after"][fields + 1, row]
        )

    def diagonal_pairs(name, count, first, starts):
        for pair in range(count):
            value = diagonal(named[name][extra + 1, pair])
            for line in range(2):
                for start in starts:
                    diagonal_ref[first + 2 * pair + line, start : start + TILE] = value[
                        line * TILE : (line + 1) * TILE
                    ]

    diagonal_pairs("below", rows // 2, own_row, (0,))
    diagonal_pairs("above", rows // 2, own_row, (above_cell,))
    diagonal_pairs("corner_before", INNER // 2, own_row - INNER, (0, above_cell))
    diagonal_pairs("corner_after", INNER // 2, own_row + rows, (0, above_cell))

    row_index = named["control"][0]
    weights = [named["coefficients"][row_index, order] for order in range(ITERS + 1)]

    if slot == 0:
        sum_ref[...] = jnp.zeros_like(sum_ref)
    else:
        sum_ref[...] = named["density"][...]

    def one_field(f, carry):
        def reader(ref, offset):
            def read(row, start, count):
                first = start + offset
                if first % TILE:
                    first = first + zero_shift
                return ref[row, pl.ds(first, count)]

            return read

        read0 = reader(t0_ref.at[f], 0)
        read1 = reader(t1_ref, moved)
        read2 = reader(t2_ref, moved)
        read_diagonal = reader(diagonal_ref, 0)

        def spans(outer, inner):
            first, last = own_row - outer, own_row + rows + outer
            narrow, wide = (own_cell, depth), (own_cell - half, middle)
            inner_first, inner_last = own_row - inner, own_row + rows + inner
            groups = [(list(range(first, inner_first)), narrow)]
            for row in range(inner_first, inner_last, GROUP):
                groups.append((list(range(row, min(row + GROUP, inner_last))), wide))
            groups.append((list(range(inner_last, last)), narrow))
            return [(lines, span) for lines, span in groups if lines]

        def sweep(read, groups, finish):
            window, window_span = {}, None
            for lines, span in groups:
                if span != window_span:
                    window, window_span = {}, span
                start, count = span
                for row in range(lines[0] - REACH, lines[-1] + REACH + 1):
                    if row not in window:
                        window[row] = read(row, start, count)
                results = []
                for row in lines:
                    centre = window[row]
                    near = pltpu.roll(centre, 1, 1) + pltpu.roll(centre, lanes - 1, 1)
                    far = pltpu.roll(centre, 2, 1) + pltpu.roll(centre, lanes - 2, 1)
                    near = near + (window[row - 1] + window[row + 1])
                    far = far + (window[row - 2] + window[row + 2])
                    near = near + (read(row, start - 1, count) + read(row, start + 1, count))
                    far = far + (read(row, start - 2, count) + read(row, start + 2, count))
                    value = read_diagonal(row, start, count) * centre
                    value = value + (near_scale * near + far_scale * far)
                    results.append(finish(row, start, count, centre, value))
                for row, (store, result) in zip(lines, results):
                    store(row, result)
                for row in [row for row in window if row < lines[-1] + 1 - REACH]:
                    del window[row]

        def store_to(ref, start, count):
            def store(row, value):
                ref[row, pl.ds(start + moved, count)] = value

            return store

        def first_result(row, start, count, centre, value):
            return store_to(t1_ref, start, count), 0.5 * value

        def second_result(row, start, count, centre, value):
            return store_to(t2_ref, start, count), value - read0(row, start, count)

        def last_result(row, start, count, centre, value):
            first = read1(row, start, count)
            answer = weights[0] * read0(row, start, count) + weights[1] * first
            answer = answer + (weights[2] * centre + weights[3] * (value - first))
            answer = answer.astype(bf16)
            line = row - own_row
            added = sum_ref[line] + answer.astype(f32) * field_ref[0, f, line].astype(f32)

            def store(row, pair):
                response_ref[0, f, line] = pair[0]
                sum_ref[line] = pair[1]

            return store, (answer, added)

        sweep(read0, spans(INNER, INNER - REACH), first_result)
        sweep(read1, spans(REACH, 0), second_result)
        lines = range(own_row, own_row + rows)
        narrow = (own_cell, depth)
        groups = [(list(lines[at : at + GROUP]), narrow) for at in range(0, rows, GROUP)]
        sweep(read2, groups, last_result)
        return carry

    lax.fori_loop(0, fields, one_field, 0)

    if not last_slot:
        density_refs[0][...] = sum_ref[...]
        return
    total = sum_ref[...] * scale
    if not split:
        density_refs[0][...] = total
        return
    turned = pltpu.roll(total, lanes // 2, 2)
    total = jnp.where(named["control"][2] == 0, total, turned)
    density_refs[0][...] = total
    upper, lower = total[:, : depth // 2], total[:, depth // 2 :]
    lane = lax.broadcasted_iota(jnp.int32, upper.shape, 2)
    density_refs[1][...] = jnp.where(lane < lanes // 2, pltpu.roll(upper, lanes // 2, 2), lower)


DEEP_NAMES = ("below", "above", "corner_before", "corner_after")


def chain(slot, orbitals, partner, halos, partner_halos, perturb, local_pot, coefficients, control,
          matrices, scale, split, carried):
    slots, fields, rows, depth, lanes = orbitals.shape
    same = partner is None
    names, operands, specs = [], [], []
    last_slot = slot == slots - 1

    def add(name, value, spec):
        names.append(name)
        operands.append(value)
        specs.append(spec)

    block = (1, fields, rows, depth, lanes)
    at_slot = pl.BlockSpec(block, lambda step: (slot, 0, 0, 0, 0))

    def add_halos(prefix, halos):
        row_halos, deep_halos = halos[0], halos[1]
        for name, value in zip(("before", "after"), row_halos[slot]):
            add(prefix + name, value, whole())
        for name, value in zip(DEEP_NAMES, deep_halos):
            add(prefix + name, value, whole())

    add("field", orbitals, at_slot)
    add_halos("", halos)
    if slot:
        for name, value in zip(("before", "after"), halos[0][0]):
            add("kick_" + name, value, whole())
    if not same:
        add("partner_field", partner, at_slot)
        add_halos("partner_", partner_halos)
    add("perturb", perturb, whole())
    add("local_pot", local_pot, whole())
    add("coefficients", coefficients, in_smem())
    add("control", control, in_smem())
    matrix = pl.BlockSpec((1,) + matrices[0].shape[1:], lambda step: (slot, 0, 0))
    add("high", matrices[0], matrix)
    add("low", matrices[1], matrix)
    aliases = {}
    if slot:
        add("density", carried[1], whole())
        aliases = {len(names): 0}
        add("response", carried[0], pl.BlockSpec(memory_space=pl.ANY))

    density_shapes = [jax.ShapeDtypeStruct((rows, depth, lanes), f32)]
    if last_slot and split:
        density_shapes.append(jax.ShapeDtypeStruct((rows, depth // 2, lanes), f32))

    def kernel(*refs):
        named = dict(zip(names, refs))
        if not slot:
            named["kick_before"] = named["before"]
            named["kick_after"] = named["after"]
        outs = refs[len(names) : len(names) + 1 + len(density_shapes)]
        scratch = refs[len(names) + len(outs) :]
        chain_kernel(slot, same, scale, last_slot, split, named, outs[0], outs[1:], scratch)

    long_rows = rows + 2 * WIDE
    long_depth = depth + 2 * TILE
    return pl.pallas_call(
        kernel,
        grid=(1,),
        out_shape=(jax.ShapeDtypeStruct(orbitals.shape, bf16), *density_shapes),
        in_specs=specs,
        out_specs=(at_slot,) + (whole(),) * len(density_shapes),
        scratch_shapes=[
            pltpu.VMEM((fields, long_rows, long_depth, lanes), f32),
            pltpu.VMEM((long_rows, long_depth + TILE, lanes), f32),
            pltpu.VMEM((long_rows, long_depth + TILE, lanes), f32),
            pltpu.VMEM((long_rows, long_depth, lanes), f32),
            pltpu.VMEM((rows, depth, lanes), f32),
        ],
        input_output_aliases=aliases,
        compiler_params=params(),
        cost_estimate=NO_COST,
        name="response_chain",
    )(*operands)


def from_behind(value, axis, steps):
    count = lax.axis_size(axis)
    pairs = [(source, (source + steps) % count) for source in range(count)]
    return lax.ppermute(value, axis, pairs)


def route(blocks, shift_count):
    groups = lax.axis_size("ka")
    if groups == 2:
        return from_behind(blocks, "ka", -1)
    moved = blocks
    for bit_index in range((groups - 1).bit_length()):
        shifted = from_behind(moved, "ka", -(1 << bit_index))
        taken = shift_count >> bit_index & 1 == 1
        moved = jnp.where(taken, shifted, moved)
    return moved


def finish_kernel(total_ref, other_ref, out_ref):
    total = total_ref[...]
    other = other_ref[...]
    lanes = total.shape[2]
    depth = total.shape[1]
    kept = lanes // 2
    out_ref[:, : depth // 2] = (total[:, : depth // 2] + other)[:, :, :kept]
    out_ref[:, depth // 2 :] = (total[:, depth // 2 :] + pltpu.roll(other, kept, 2))[:, :, :kept]


def finish(total, packed):
    other = from_behind(packed, "ka", 1)
    rows, depth, lanes = total.shape
    return pl.pallas_call(
        finish_kernel,
        out_shape=jax.ShapeDtypeStruct((rows, depth, lanes // 2), f32),
        in_specs=[whole(), whole()],
        out_specs=whole(),
        compiler_params=params(),
        cost_estimate=NO_COST,
        name="density_sum",
    )(total, other)


def body(orbitals, coefficients, local_pot, perturb, q_index):
    groups = lax.axis_size("ka")
    shift_count = q_index[0] % groups
    group_index = lax.axis_index("ka")
    slots, bands, parts, rows, depth, lanes = orbitals.shape
    fields = orbitals.reshape((slots, bands * parts, rows, depth, lanes))
    partner_group = (group_index + shift_count) % groups
    scale = 2.0 / (slots * groups)
    split = groups == 2

    def work(shifted):
        halos = exchange(fields, (perturb, local_pot))
        partner, partner_halos = None, None
        if shifted:
            partner = route(fields, shift_count)
            partner_halos = exchange(partner)
        pieces = inner_products(fields, perturb, partner)
        matrices = factors(pieces, slots, bands * parts, depth)
        carried = None
        for slot in range(slots):
            row_index = partner_group * slots + slot
            control = jnp.stack([row_index, jnp.zeros_like(row_index), group_index])
            carried = chain(
                slot, fields, partner, halos, partner_halos, perturb, local_pot, coefficients,
                control.astype(jnp.int32), matrices, scale, split, carried,
            )
        if split:
            return carried[0], finish(carried[1], carried[2])
        return carried[0], lax.psum_scatter(carried[1], "ka", scatter_dimension=2, tiled=True)

    responses, density = lax.cond(shift_count == 0, lambda: work(False), lambda: work(True))
    return responses.reshape(orbitals.shape), density


def solution(mesh):
    return jax.shard_map(
        body,
        mesh=mesh,
        in_specs=(
            P("ka", None, None, "sy", "sz", None),
            P(),
            P("sy", "sz", None),
            P("sy", "sz", None),
            P(),
        ),
        out_specs=(P("ka", None, None, "sy", "sz", None), P("sy", "sz", "ka")),
        check_vma=False,
    )
```

```python
import functools

import jax
import jax.numpy as jnp
from jax import lax
from jax.experimental import pallas as pl
from jax.experimental.pallas import tpu as pltpu
from jax.sharding import PartitionSpec as P

ITERS = 3
REACH = 2
WIDE = REACH * ITERS
INNER = WIDE - REACH
TILE = 8

centre_weight = -7.5
near_weight = 4.0 / 3.0
far_weight = -1.0 / 12.0
norm_epsilon = 1e-06

near_scale = 0.4 * -0.5 * near_weight
far_scale = 0.4 * -0.5 * far_weight

f32 = jnp.float32
bf16 = jnp.bfloat16

VMEM_LIMIT = 40 * 1024 * 1024
RUN = 8
NO_COST = pl.CostEstimate(flops=0, transcendentals=0, bytes_accessed=0)


def params():
    return pltpu.CompilerParams(vmem_limit_bytes=VMEM_LIMIT)


def whole():
    return pl.BlockSpec(memory_space=pltpu.VMEM)


def in_smem():
    return pl.BlockSpec(memory_space=pltpu.SMEM)


def pack_kernel(slots, fields, extras, *refs):
    block_refs = refs[: 1 + extras]
    up_ref, down_ref, deep_up_ref, deep_down_ref, token_ref = refs[1 + extras :]
    token_ref[...] = jnp.zeros_like(token_ref)
    rows, depth = block_refs[0].shape[-3:-1]

    def put(read, slab_index, deep_index):
        if slab_index is not None:
            up_ref[slab_index] = read(rows - WIDE, WIDE).astype(bf16)
            down_ref[slab_index] = read(0, WIDE).astype(bf16)
        for pair in range(rows // 2):
            first = read(2 * pair, 1)[0].astype(f32)
            second = read(2 * pair + 1, 1)[0].astype(f32)
            deep_up_ref[deep_index, pair] = jnp.concatenate(
                [first[depth - TILE :], second[depth - TILE :]], 0
            ).astype(bf16)
            deep_down_ref[deep_index, pair] = jnp.concatenate(
                [first[:TILE], second[:TILE]], 0
            ).astype(bf16)

    for slot in range(slots):

        def one(field, carry, slot=slot):
            put(
                lambda start, count: block_refs[0][slot, field, pl.ds(start, count)],
                None if slot else field,
                slot * fields + field,
            )
            return carry

        lax.fori_loop(0, fields, one, 0)
    for index in range(extras):
        ref = block_refs[1 + index]
        put(
            lambda start, count, ref=ref: ref[pl.ds(start, count)],
            fields + index,
            slots * fields + index,
        )


def pack(blocks, extras):
    slots, fields, rows, depth, lanes = blocks.shape
    count = fields + len(extras)
    shapes = [jax.ShapeDtypeStruct((count, WIDE, depth, lanes), bf16)] * 2
    total = slots * fields + len(extras)
    shapes += [jax.ShapeDtypeStruct((total, rows // 2, 2 * TILE, lanes), bf16)] * 2
    shapes += [jax.ShapeDtypeStruct((TILE, lanes), f32)]
    return pl.pallas_call(
        functools.partial(pack_kernel, slots, fields, len(extras)),
        out_shape=tuple(shapes),
        in_specs=[whole()] * (1 + len(extras)),
        out_specs=(whole(),) * len(shapes),
        compiler_params=params(),
        cost_estimate=NO_COST,
        name="pack_halos",
    )(blocks, *extras)


def pack_rows_kernel(block_ref, *refs):
    up_ref, down_ref = refs[-2:]
    rows = block_ref.shape[2]
    up_ref[...] = block_ref[0, :, rows - WIDE :]
    down_ref[...] = block_ref[0, :, :WIDE]


def pack_rows(blocks, slot, after):
    _, fields, rows, depth, lanes = blocks.shape
    shape = jax.ShapeDtypeStruct((fields, WIDE, depth, lanes), bf16)
    block = pl.BlockSpec((1, fields, rows, depth, lanes), lambda step: (slot, 0, 0, 0, 0))
    return pl.pallas_call(
        pack_rows_kernel,
        grid=(1,),
        out_shape=(shape, shape),
        in_specs=[block] + [pl.BlockSpec(memory_space=pl.ANY)] * len(after),
        out_specs=(whole(), whole()),
        compiler_params=params(),
        cost_estimate=NO_COST,
        name="pack_rows",
    )(blocks, *after)


def to_next(value, axis):
    size = lax.axis_size(axis)
    return lax.ppermute(value, axis, [(i, (i + 1) % size) for i in range(size)])


def to_previous(value, axis):
    size = lax.axis_size(axis)
    return lax.ppermute(value, axis, [((i + 1) % size, i) for i in range(size)])


def exchange(blocks, extras=()):
    slots = blocks.shape[0]
    up, down, deep_up, deep_down, token = pack(blocks, extras)
    rows = [(to_next(up, "sy"), to_previous(down, "sy"))]
    for slot in range(1, slots):
        up, down = pack_rows(blocks, slot, rows[-1])
        rows.append((to_next(up, "sy"), to_previous(down, "sy")))
    below = to_next(deep_up, "sz")
    above = to_previous(deep_down, "sz")
    first_half = (lax.broadcasted_iota(jnp.int32, below.shape, 2) % TILE) < TILE // 2
    corner = jnp.where(first_half, above, below)
    pairs = INNER // 2
    corner_before = to_next(corner[:, corner.shape[1] - pairs :], "sy")
    corner_after = to_previous(corner[:, :pairs], "sy")
    return rows, (below, above, corner_before, corner_after), token


def inner_kernel(same, *refs):
    field_ref, perturb_ref, out_ref = refs[0], refs[-3 if same else -2], refs[-1]
    partner_ref = field_ref if same else refs[1]
    slots, fields, rows, depth, lanes = field_ref.shape
    size = fields * depth
    row_of = lax.broadcasted_iota(jnp.int32, (size, size), 0)
    lane_of = lax.broadcasted_iota(jnp.int32, (size, size), 1)
    same_cell = row_of % depth == lane_of % depth
    gather = (
        lax.broadcasted_iota(jnp.int32, (size, lanes), 0) // depth
        == lax.broadcasted_iota(jnp.int32, (size, lanes), 1)
    ).astype(f32)
    lane = lax.broadcasted_iota(jnp.int32, (fields, lanes), 1)
    for slot in range(slots):
        lefts, rights = [], []
        norms = jnp.zeros((fields, depth, lanes), f32)
        for row in range(rows):
            partner = partner_ref[slot, :, row]
            wide = partner.astype(f32)
            norms = norms + wide * wide
            raw = wide if same else field_ref[slot, :, row].astype(f32)
            source = perturb_ref[row][None] * raw
            high = source.astype(bf16)
            low = (source - high.astype(f32)).astype(bf16)
            lefts += [partner.reshape((size, lanes))] * 2
            rights += [high.reshape((size, lanes)), low.reshape((size, lanes))]
        products = lax.dot_general(
            jnp.concatenate(lefts, 1),
            jnp.concatenate(rights, 1),
            (((1,), (1,)), ((), ())),
            preferred_element_type=f32,
        )
        products = jnp.where(same_cell, products, 0.0).reshape((fields, depth, size))
        products = jnp.sum(products, axis=1)
        products = jnp.dot(
            products, gather, precision=lax.Precision.HIGHEST, preferred_element_type=f32
        )
        norm = jnp.sum(jnp.sum(norms, axis=1), axis=1, keepdims=True)
        out_ref[slot] = jnp.where(lane == fields, norm, products)


def pair_sum(value, axis):
    size = lax.axis_size(axis)
    if size & (size - 1):
        return lax.psum(value, axis)
    step = 1
    while step < size:
        value = value + lax.ppermute(value, axis, [(i, i ^ step) for i in range(size)])
        step *= 2
    return value


def inner_products(orbitals, perturb, partners, after):
    slots, fields, _, _, lanes = orbitals.shape
    same = partners is None
    operands = (orbitals, perturb, after) if same else (orbitals, partners, perturb)
    specs = [whole()] * 2 + [pl.BlockSpec(memory_space=pl.ANY) if same else whole()]
    local = pl.pallas_call(
        functools.partial(inner_kernel, same),
        out_shape=jax.ShapeDtypeStruct((slots, fields, lanes), f32),
        in_specs=specs,
        out_specs=whole(),
        compiler_params=params(),
        cost_estimate=NO_COST,
        name="inner_products",
    )(*operands)
    return pair_sum(pair_sum(local, "sy"), "sz")


def factor_kernel(fields, depth, sums_ref, factor_ref, turn_ref, back_ref, spread_ref):
    size = fields * depth
    slots, _, lanes = sums_ref.shape
    row = lax.broadcasted_iota(jnp.int32, (fields, lanes), 0)
    lane = lax.broadcasted_iota(jnp.int32, (fields, lanes), 1)
    wide_lane = lax.broadcasted_iota(jnp.int32, (fields, size), 1)
    expand = (
        lax.broadcasted_iota(jnp.int32, (lanes, size), 1) // depth
        == lax.broadcasted_iota(jnp.int32, (lanes, size), 0)
    ).astype(f32)

    def swap_rows(value):
        return jnp.where(
            row % 2 == 0, pltpu.roll(value, fields - 1, 0), pltpu.roll(value, 1, 0)
        )

    def swap_lanes(value):
        return jnp.where(
            lane % 2 == 0, pltpu.roll(value, lanes - 1, 1), pltpu.roll(value, 1, 1)
        )

    for slot in range(slots):
        sums = sums_ref[slot]
        across = swap_rows(swap_lanes(sums))
        both = jnp.where((row + lane) % 2 == 0, sums + across, sums - across)
        norm = sums + swap_rows(sums)
        norm = jnp.sum(jnp.where(lane == fields, norm, 0.0), axis=1, keepdims=True)
        both = jnp.where(lane < fields, both / (norm + norm_epsilon), 0.0)
        both = jnp.concatenate([both, jnp.zeros((lanes - fields, lanes), f32)], 0)
        by_out = -jnp.transpose(both)[:fields]
        by_out = jnp.dot(
            by_out, expand, precision=lax.Precision.HIGHEST, preferred_element_type=f32
        )
        high = by_out.astype(bf16).astype(f32)
        low = by_out - high
        for cell in range(0, depth, 2):
            at = pl.ds(cell * fields, 2 * fields)
            for part, value in enumerate((high, low)):
                lines = [
                    jnp.where(wide_lane % depth == each, value, 0.0) for each in (cell, cell + 1)
                ]
                factor_ref[slot, at, pl.ds(part * size, size)] = jnp.concatenate(lines, 0).astype(
                    bf16
                )
    first = lax.broadcasted_iota(jnp.int32, (size, size), 0)
    second = lax.broadcasted_iota(jnp.int32, (size, size), 1)
    turn = (first // fields == second % depth) & (first % fields == second // depth)
    turn_ref[...] = turn.astype(f32).astype(bf16)
    back = (first // depth == second % fields) & (first % depth == second // fields)
    back_ref[...] = back.astype(f32).astype(bf16)
    first = lax.broadcasted_iota(jnp.int32, spread_ref.shape, 0)
    second = lax.broadcasted_iota(jnp.int32, spread_ref.shape, 1)
    spread_ref[...] = (first // fields == second % depth).astype(f32).astype(bf16)


def factors(sums, depth):
    slots, fields, _ = sums.shape
    size = fields * depth
    square = jax.ShapeDtypeStruct((size, size), bf16)
    return pl.pallas_call(
        functools.partial(factor_kernel, fields, depth),
        out_shape=(
            jax.ShapeDtypeStruct((slots, size, 2 * size), bf16),
            square,
            square,
            jax.ShapeDtypeStruct((size, 3 * depth), bf16),
        ),
        in_specs=[whole()],
        out_specs=(whole(),) * 4,
        compiler_params=params(),
        cost_estimate=NO_COST,
        name="projection_factors",
    )(sums)


def three_parts(value):
    high = value.astype(bf16)
    rest = value - high.astype(f32)
    middle = rest.astype(bf16)
    return [high, middle, (rest - middle.astype(f32)).astype(bf16)]


def chain_kernel(slot, same, scale, last_slot, split, named, response_ref, density_refs, scratch):
    t0_ref, t1_ref, t2_ref, diagonal_ref, sum_ref = scratch
    field_ref = named["field"]
    fields, rows, depth, lanes = field_ref.shape[1:]
    own = WIDE
    size = fields * depth
    turned = (depth, fields, lanes)
    factor = named["factor"][0]
    turn = named["turn"][...]
    spread = named["spread"][...]

    def dot(matrix, parts):
        return jnp.dot(matrix, jnp.concatenate(parts, 1), preferred_element_type=f32)

    def spread_out(values):
        if values[0].dtype == bf16:
            return dot(spread[:, :depth], values)
        return dot(spread, [jnp.concatenate(three_parts(value), 0) for value in values])

    def block_of(value, index):
        return value[:, index * lanes : (index + 1) * lanes].reshape(turned)

    def project(pieces):
        raws = [raw.reshape((size, lanes)) for raw, _, _, _ in pieces]
        others = raws if same else [partner.reshape((size, lanes)) for _, partner, _, _ in pieces]
        along = dot(factor, [jnp.concatenate([other, other], 0) for other in others])
        moved = dot(turn, raws)
        kick = spread_out([kick for _, _, kick, _ in pieces])
        value = kick * moved + along
        for index, (_, _, _, write) in enumerate(pieces):
            write(block_of(value, index))

    partner_own = (lambda row: None) if same else (lambda row: named["partner_field"][0, :, row])
    partner_halo = (
        (lambda name, index: None) if same else (lambda name, index: named["partner_" + name][index])
    )
    own_cells = pl.ds(own, depth)

    def inside(pair, carry):
        def piece(row):
            def write(value):
                t0_ref[own + row, own_cells] = value

            return field_ref[0, :, row], partner_own(row), named["perturb"][row], write

        project([piece(2 * pair), piece(2 * pair + 1)])
        return carry

    lax.fori_loop(0, rows // 2, inside, 0)

    def outer(row, carry):
        def piece(name, first):
            def write(value):
                t0_ref[first + row, own_cells] = value

            index = (pl.ds(0, fields), row)
            kick = named["kick_" + name][fields, row]
            return named[name][index], partner_halo(name, index), kick, write

        project([piece("before", 0), piece("after", own + rows)])
        return carry

    lax.fori_loop(0, WIDE, outer, 0)

    pairs = depth // (2 * TILE)
    lines = 2 * pairs
    extra = named["below"].shape[0] - 2
    above = own + depth

    def write_lines(ref, first, places):
        def write(value):
            for line in range(lines):
                for target, source, count in places:
                    source = line * TILE + source
                    ref[first + line, pl.ds(target, count)] = value[source : source + count]

        return write

    below_places = ((0, TILE - WIDE, WIDE),)
    above_places = ((above, 0, WIDE),)
    corner_places = ((own - TILE // 2, TILE // 2, TILE // 2), (above, 0, TILE // 2))

    def deep(group, names, firsts, places):
        def piece(name, first, places):
            index = (pl.ds(slot * fields, fields), pl.ds(group * pairs, pairs))
            partner = partner_halo(name, index)
            kick = named[name][extra, pl.ds(group * pairs, pairs)].reshape((depth, lanes))
            write = write_lines(t0_ref, first + lines * group, places)
            return named[name][index], partner, kick, write

        project([piece(*each) for each in zip(names, firsts, places)])

    def deep_inside(group, carry):
        deep(group, ("below", "above"), (own, own), (below_places, above_places))
        return carry

    lax.fori_loop(0, rows // lines, deep_inside, 0)
    for group in range(INNER // lines):
        deep(
            group,
            ("corner_before", "corner_after"),
            (own - INNER, own + rows),
            (corner_places, corner_places),
        )

    def diagonal(values):
        return 0.4 * (spread_out(values) - 0.5 * centre_weight) - 2.0

    def diagonal_inside(pair, carry):
        value = diagonal([named["local_pot"][2 * pair], named["local_pot"][2 * pair + 1]])
        for index in range(2):
            diagonal_ref[own + 2 * pair + index, own_cells] = block_of(value, index)
        return carry

    lax.fori_loop(0, rows // 2, diagonal_inside, 0)

    def diagonal_outer(row, carry):
        value = diagonal(
            [
                named["kick_before"][fields + 1, WIDE - INNER + row],
                named["kick_after"][fields + 1, row],
            ]
        )
        diagonal_ref[own - INNER + row, own_cells] = block_of(value, 0)
        diagonal_ref[own + rows + row, own_cells] = block_of(value, 1)
        return carry

    lax.fori_loop(0, INNER, diagonal_outer, 0)

    def diagonal_deep(group, names, firsts, places):
        at = (extra + 1, pl.ds(group * pairs, pairs))
        value = diagonal([named[name][at].reshape((depth, lanes)) for name in names])
        for index in range(2):
            write_lines(diagonal_ref, firsts[index] + lines * group, places[index])(
                block_of(value, index)
            )

    for group in range(rows // lines):
        diagonal_deep(group, ("below", "above"), (own, own), (below_places, above_places))
    for group in range(INNER // lines):
        diagonal_deep(
            group,
            ("corner_before", "corner_after"),
            (own - INNER, own + rows),
            (corner_places, corner_places),
        )

    row_index = named["control"][0]
    weights = [named["coefficients"][row_index, order] for order in range(ITERS + 1)]

    def twice(ref, row, start, count):
        line = ref[row, pl.ds(start - REACH, count + 2 * REACH)]
        centre = line[REACH : REACH + count]
        near = pltpu.roll(centre, 1, 2) + pltpu.roll(centre, lanes - 1, 2)
        far = pltpu.roll(centre, 2, 2) + pltpu.roll(centre, lanes - 2, 2)
        cells = pl.ds(start, count)
        near = near + (line[REACH - 1 : REACH - 1 + count] + line[REACH + 1 : REACH + 1 + count])
        far = far + (line[:count] + line[2 * REACH :])
        near = near + (ref[row - 1, cells] + ref[row + 1, cells])
        far = far + (ref[row - 2, cells] + ref[row + 2, cells])
        value = diagonal_ref[row, cells] * centre + (near_scale * near + far_scale * far)
        return centre, value

    def sweep(ref, first, last, wide, finish):
        def one(row, carry):
            start, end = own - wide, own + depth + wide
            while start < end:
                count = min(RUN, end - start)
                finish(row, start, count, *twice(ref, row, start, count))
                start += count
            return carry

        lax.fori_loop(first, last, one, 0)

    def first_result(row, start, count, centre, value):
        t1_ref[row, pl.ds(start, count)] = 0.5 * value

    def second_result(row, start, count, centre, value):
        cells = pl.ds(start, count)
        t2_ref[row, cells] = value - t0_ref[row, cells]

    end = own + rows
    for wide in range(INNER, -1, -REACH):
        reach = INNER - wide
        if reach == 0:
            sweep(t0_ref, own, end, wide, first_result)
        else:
            sweep(t0_ref, own - reach, own - reach + REACH, wide, first_result)
            sweep(t0_ref, end + reach - REACH, end + reach, wide, first_result)
    sweep(t1_ref, own, end, REACH, second_result)
    sweep(t1_ref, own - REACH, own, 0, second_result)
    sweep(t1_ref, end, end + REACH, 0, second_result)

    if slot == 0:
        sum_ref[...] = jnp.zeros_like(sum_ref)
    else:
        sum_ref[...] = named["density"][...]
    back = named["back"][...]

    def last_sweep(pair, carry):
        answers = []
        for index in range(2):
            row = own + 2 * pair + index
            pieces = []
            for start in range(own, own + depth, RUN):
                count = min(RUN, own + depth - start)
                cells = pl.ds(start, count)
                second, value = twice(t2_ref, row, start, count)
                first = t1_ref[row, cells]
                answer = weights[0] * t0_ref[row, cells] + weights[1] * first
                answer = answer + (weights[2] * second + weights[3] * (value - first))
                pieces.append(answer.reshape((count * fields, lanes)).astype(bf16))
            answers.append(jnp.concatenate(pieces, 0))
        answer = dot(back, answers)
        for index in range(2):
            line = 2 * pair + index
            part = answer[:, index * lanes : (index + 1) * lanes].reshape((fields, depth, lanes))
            response_ref[0, :, line] = part.astype(bf16)
            sum_ref[line] += jnp.sum(part * field_ref[0, :, line].astype(f32), axis=0)
        return carry

    lax.fori_loop(0, rows // 2, last_sweep, 0)

    if not last_slot:
        density_refs[0][...] = sum_ref[...]
        return
    total = sum_ref[...] * scale
    if not split:
        density_refs[0][...] = total
        return
    turned = pltpu.roll(total, lanes // 2, 2)
    total = jnp.where(named["control"][1] == 0, total, turned)
    density_refs[0][...] = total
    upper, lower = total[:, : depth // 2], total[:, depth // 2 :]
    lane = lax.broadcasted_iota(jnp.int32, upper.shape, 2)
    density_refs[1][...] = jnp.where(lane < lanes // 2, pltpu.roll(upper, lanes // 2, 2), lower)


DEEP_NAMES = ("below", "above", "corner_before", "corner_after")


def chain(slot, orbitals, partner, halos, partner_halos, perturb, local_pot, coefficients, control,
          matrices, scale, split, carried):
    slots, fields, rows, depth, lanes = orbitals.shape
    same = partner is None
    names, operands, specs = [], [], []
    last_slot = slot == slots - 1

    def add(name, value, spec):
        names.append(name)
        operands.append(value)
        specs.append(spec)

    block = (1, fields, rows, depth, lanes)
    at_slot = pl.BlockSpec(block, lambda step: (slot, 0, 0, 0, 0))

    def add_halos(prefix, halos):
        row_halos, deep_halos = halos[0], halos[1]
        for name, value in zip(("before", "after"), row_halos[slot]):
            add(prefix + name, value, whole())
        for name, value in zip(DEEP_NAMES, deep_halos):
            add(prefix + name, value, whole())

    add("field", orbitals, at_slot)
    add_halos("", halos)
    if slot:
        for name, value in zip(("before", "after"), halos[0][0]):
            add("kick_" + name, value, whole())
    if not same:
        add("partner_field", partner, at_slot)
        add_halos("partner_", partner_halos)
    add("perturb", perturb, whole())
    add("local_pot", local_pot, whole())
    add("coefficients", coefficients, in_smem())
    add("control", control, in_smem())
    add("factor", matrices[0], pl.BlockSpec((1,) + matrices[0].shape[1:], lambda step: (slot, 0, 0)))
    for name, value in zip(("turn", "back", "spread"), matrices[1:]):
        add(name, value, whole())
    aliases = {}
    if slot:
        add("density", carried[1], whole())
        aliases = {len(names): 0}
        add("response", carried[0], pl.BlockSpec(memory_space=pl.ANY))

    density_shapes = [jax.ShapeDtypeStruct((rows, depth, lanes), f32)]
    if last_slot and split:
        density_shapes.append(jax.ShapeDtypeStruct((rows, depth // 2, lanes), f32))

    def kernel(*refs):
        named = dict(zip(names, refs))
        if not slot:
            named["kick_before"] = named["before"]
            named["kick_after"] = named["after"]
        outs = refs[len(names) : len(names) + 1 + len(density_shapes)]
        scratch = refs[len(names) + len(outs) :]
        chain_kernel(slot, same, scale, last_slot, split, named, outs[0], outs[1:], scratch)

    long_block = (rows + 2 * WIDE, depth + 2 * WIDE, fields, lanes)
    return pl.pallas_call(
        kernel,
        grid=(1,),
        out_shape=(jax.ShapeDtypeStruct(orbitals.shape, bf16), *density_shapes),
        in_specs=specs,
        out_specs=(at_slot,) + (whole(),) * len(density_shapes),
        scratch_shapes=[
            pltpu.VMEM(long_block, f32),
            pltpu.VMEM(long_block, f32),
            pltpu.VMEM(long_block, f32),
            pltpu.VMEM(long_block, f32),
            pltpu.VMEM((rows, depth, lanes), f32),
        ],
        input_output_aliases=aliases,
        compiler_params=params(),
        cost_estimate=NO_COST,
        name="response_chain",
    )(*operands)


def from_behind(value, axis, steps):
    count = lax.axis_size(axis)
    pairs = [(source, (source + steps) % count) for source in range(count)]
    return lax.ppermute(value, axis, pairs)


def route(blocks, shift_count):
    groups = lax.axis_size("ka")
    if groups == 2:
        return from_behind(blocks, "ka", -1)
    moved = blocks
    for bit_index in range((groups - 1).bit_length()):
        shifted = from_behind(moved, "ka", -(1 << bit_index))
        taken = shift_count >> bit_index & 1 == 1
        moved = jnp.where(taken, shifted, moved)
    return moved


def finish_kernel(total_ref, other_ref, out_ref):
    total = total_ref[...]
    other = other_ref[...]
    lanes = total.shape[2]
    depth = total.shape[1]
    kept = lanes // 2
    out_ref[:, : depth // 2] = (total[:, : depth // 2] + other)[:, :, :kept]
    out_ref[:, depth // 2 :] = (total[:, depth // 2 :] + pltpu.roll(other, kept, 2))[:, :, :kept]


def finish(total, packed):
    other = from_behind(packed, "ka", 1)
    rows, depth, lanes = total.shape
    return pl.pallas_call(
        finish_kernel,
        out_shape=jax.ShapeDtypeStruct((rows, depth, lanes // 2), f32),
        in_specs=[whole(), whole()],
        out_specs=whole(),
        compiler_params=params(),
        cost_estimate=NO_COST,
        name="density_sum",
    )(total, other)


def body(orbitals, coefficients, local_pot, perturb, q_index):
    groups = lax.axis_size("ka")
    shift_count = q_index[0] % groups
    group_index = lax.axis_index("ka")
    slots, bands, parts, rows, depth, lanes = orbitals.shape
    fields = orbitals.reshape((slots, bands * parts, rows, depth, lanes))
    partner_group = (group_index + shift_count) % groups
    scale = 2.0 / (slots * groups)
    split = groups == 2

    def work(shifted):
        halos = exchange(fields, (perturb, local_pot))
        partner, partner_halos = None, None
        if shifted:
            partner = route(fields, shift_count)
            partner_halos = exchange(partner)
        after = None if shifted else from_behind(halos[2], "ka", 1)
        sums = inner_products(fields, perturb, partner, after)
        matrices = factors(sums, depth)
        carried = None
        for slot in range(slots):
            row_index = partner_group * slots + slot
            control = jnp.stack([row_index, group_index])
            carried = chain(
                slot, fields, partner, halos, partner_halos, perturb, local_pot, coefficients,
                control.astype(jnp.int32), matrices, scale, split, carried,
            )
        if split:
            return carried[0], finish(carried[1], carried[2])
        return carried[0], lax.psum_scatter(carried[1], "ka", scatter_dimension=2, tiled=True)

    responses, density = lax.cond(shift_count == 0, lambda: work(False), lambda: work(True))
    return responses.reshape(orbitals.shape), density


def solution(mesh):
    return jax.shard_map(
        body,
        mesh=mesh,
        in_specs=(
            P("ka", None, None, "sy", "sz", None),
            P(),
            P("sy", "sz", None),
            P("sy", "sz", None),
            P(),
        ),
        out_specs=(P("ka", None, None, "sy", "sz", None), P("sy", "sz", "ka")),
        check_vma=False,
    )
```

```python
import functools

import jax
import jax.numpy as jnp
from jax import lax
from jax.experimental import pallas as pl
from jax.experimental.pallas import tpu as pltpu
from jax.sharding import PartitionSpec as P

ITERS = 3
REACH = 2
WIDE = REACH * ITERS
INNER = WIDE - REACH
TILE = 8

centre_weight = -7.5
near_weight = 4.0 / 3.0
far_weight = -1.0 / 12.0
norm_epsilon = 1e-06

near_scale = 0.4 * -0.5 * near_weight
far_scale = 0.4 * -0.5 * far_weight

f32 = jnp.float32
bf16 = jnp.bfloat16

VMEM_LIMIT = 24 * 1024 * 1024
GROUP = 4
NO_COST = pl.CostEstimate(flops=0, transcendentals=0, bytes_accessed=0)


def params():
    return pltpu.CompilerParams(vmem_limit_bytes=VMEM_LIMIT)


def whole():
    return pl.BlockSpec(memory_space=pltpu.VMEM)


def in_smem():
    return pl.BlockSpec(memory_space=pltpu.SMEM)


def pack_kernel(slots, fields, extras, split, *refs):
    block_refs = refs[: 1 + extras]
    up_ref, down_ref, deep_up_ref, deep_down_ref, token_ref = refs[-5:]
    token_ref[...] = jnp.zeros_like(token_ref)
    rows, depth = block_refs[0].shape[-3:-1]

    def put(read, slab_index, deep_index):
        if slab_index is not None:
            up_ref[slab_index] = read(rows - WIDE, WIDE).astype(bf16)
            down_ref[slab_index] = read(0, WIDE).astype(bf16)
        for pair in range(rows // 2):
            first = read(2 * pair, 1)[0].astype(f32)
            second = read(2 * pair + 1, 1)[0].astype(f32)
            deep_up_ref[deep_index, pair] = jnp.concatenate(
                [first[depth - TILE :], second[depth - TILE :]], 0
            ).astype(bf16)
            deep_down_ref[deep_index, pair] = jnp.concatenate(
                [first[:TILE], second[:TILE]], 0
            ).astype(bf16)

    for slot in range(slots):

        def one(field, carry, slot=slot):
            put(
                lambda start, count: block_refs[0][slot, field, pl.ds(start, count)],
                (None if slot else field) if split else slot * fields + field,
                slot * fields + field,
            )
            return carry

        lax.fori_loop(0, fields, one, 0)
    for index in range(extras):
        ref = block_refs[1 + index]
        put(
            lambda start, count, ref=ref: ref[pl.ds(start, count)],
            (fields if split else slots * fields) + index,
            slots * fields + index,
        )


def pack(blocks, extras, split, after):
    slots, fields, rows, depth, lanes = blocks.shape
    count = (fields if split else slots * fields) + len(extras)
    shapes = [jax.ShapeDtypeStruct((count, WIDE, depth, lanes), bf16)] * 2
    total = slots * fields + len(extras)
    shapes += [jax.ShapeDtypeStruct((total, rows // 2, 2 * TILE, lanes), bf16)] * 2
    shapes += [jax.ShapeDtypeStruct((TILE, lanes), f32)]
    return pl.pallas_call(
        functools.partial(pack_kernel, slots, fields, len(extras), split),
        out_shape=tuple(shapes),
        in_specs=[whole()] * (1 + len(extras)) + [pl.BlockSpec(memory_space=pl.ANY)] * len(after),
        out_specs=(whole(),) * len(shapes),
        compiler_params=params(),
        cost_estimate=NO_COST,
        name="pack_halos",
    )(blocks, *extras, *after)


def pack_rows_kernel(block_ref, *refs):
    up_ref, down_ref = refs[-2:]
    rows = block_ref.shape[2]
    up_ref[...] = block_ref[0, :, rows - WIDE :]
    down_ref[...] = block_ref[0, :, :WIDE]


def pack_rows(blocks, slot, after):
    _, fields, rows, depth, lanes = blocks.shape
    shape = jax.ShapeDtypeStruct((fields, WIDE, depth, lanes), bf16)
    block = pl.BlockSpec((1, fields, rows, depth, lanes), lambda step: (slot, 0, 0, 0, 0))
    return pl.pallas_call(
        pack_rows_kernel,
        grid=(1,),
        out_shape=(shape, shape),
        in_specs=[block] + [pl.BlockSpec(memory_space=pl.ANY)] * len(after),
        out_specs=(whole(), whole()),
        compiler_params=params(),
        cost_estimate=NO_COST,
        name="pack_rows",
    )(blocks, *after)


def to_next(value, axis):
    size = lax.axis_size(axis)
    return lax.ppermute(value, axis, [(i, (i + 1) % size) for i in range(size)])


def to_previous(value, axis):
    size = lax.axis_size(axis)
    return lax.ppermute(value, axis, [((i + 1) % size, i) for i in range(size)])


def exchange(blocks, extras, split, wait_for=()):
    slots, fields = blocks.shape[:2]
    up, down, deep_up, deep_down, token = pack(blocks, extras, split, wait_for)
    before, after = to_next(up, "sy"), to_previous(down, "sy")
    below, above = to_next(deep_up, "sz"), to_previous(deep_down, "sz")
    first_half = (lax.broadcasted_iota(jnp.int32, below.shape, 2) % TILE) < TILE // 2
    corner = jnp.where(first_half, above, below)
    pairs = INNER // 2
    corner_before = to_next(corner[:, corner.shape[1] - pairs :], "sy")
    corner_after = to_previous(corner[:, :pairs], "sy")
    rows = [(before, after, slot * fields) for slot in range(1 if split else slots)]
    kick = (before, after, fields if split else slots * fields)
    return rows, (below, above, corner_before, corner_after), kick, token


def send_rows(blocks, halos, wait_for):
    rows, deep = halos[:2]
    for slot in range(len(rows), blocks.shape[0]):
        up, down = pack_rows(blocks, slot, rows[-1][:2] + deep[2:] + wait_for)
        rows.append((to_next(up, "sy"), to_previous(down, "sy"), 0))


def inner_kernel(same, *refs):
    field_ref, perturb_ref, out_ref = refs[0], refs[-3], refs[-1]
    partner_ref = field_ref if same else refs[1]
    slots, fields, rows, depth, lanes = field_ref.shape
    size = fields * depth
    row_of = lax.broadcasted_iota(jnp.int32, (size, size), 0)
    lane_of = lax.broadcasted_iota(jnp.int32, (size, size), 1)
    same_cell = row_of % depth == lane_of % depth
    gather = (
        lax.broadcasted_iota(jnp.int32, (size, lanes), 0) // depth
        == lax.broadcasted_iota(jnp.int32, (size, lanes), 1)
    ).astype(f32)
    lane = lax.broadcasted_iota(jnp.int32, (fields, lanes), 1)
    for slot in range(slots):
        lefts, rights = [], []
        norms = jnp.zeros((fields, depth, lanes), f32)
        for row in range(rows):
            partner = partner_ref[slot, :, row]
            wide = partner.astype(f32)
            norms = norms + wide * wide
            raw = wide if same else field_ref[slot, :, row].astype(f32)
            source = perturb_ref[row][None] * raw
            high = source.astype(bf16)
            low = (source - high.astype(f32)).astype(bf16)
            lefts += [partner.reshape((size, lanes))] * 2
            rights += [high.reshape((size, lanes)), low.reshape((size, lanes))]
        products = lax.dot_general(
            jnp.concatenate(lefts, 1),
            jnp.concatenate(rights, 1),
            (((1,), (1,)), ((), ())),
            preferred_element_type=f32,
        )
        products = jnp.where(same_cell, products, 0.0).reshape((fields, depth, size))
        products = jnp.sum(products, axis=1)
        products = jnp.dot(
            products, gather, precision=lax.Precision.HIGHEST, preferred_element_type=f32
        )
        norm = jnp.sum(jnp.sum(norms, axis=1), axis=1, keepdims=True)
        out_ref[slot] = jnp.where(lane == fields, norm, products)


def pair_sum(value, axis):
    size = lax.axis_size(axis)
    if size & (size - 1):
        return lax.psum(value, axis)
    step = 1
    while step < size:
        value = value + lax.ppermute(value, axis, [(i, i ^ step) for i in range(size)])
        step *= 2
    return value


def inner_products(orbitals, perturb, partners, after):
    slots, fields, _, _, lanes = orbitals.shape
    same = partners is None
    operands = (orbitals, perturb, after) if same else (orbitals, partners, perturb, after)
    specs = [whole()] * (len(operands) - 1) + [pl.BlockSpec(memory_space=pl.ANY)]
    local = pl.pallas_call(
        functools.partial(inner_kernel, same),
        out_shape=jax.ShapeDtypeStruct((slots, fields, lanes), f32),
        in_specs=specs,
        out_specs=whole(),
        compiler_params=params(),
        cost_estimate=NO_COST,
        name="inner_products",
    )(*operands)
    return pair_sum(pair_sum(local, "sy"), "sz")


def factor_kernel(fields, depth, sums_ref, factor_ref, lanes_ref):
    size = fields * depth
    slots, _, lanes = sums_ref.shape
    row = lax.broadcasted_iota(jnp.int32, (fields, lanes), 0)
    lane = lax.broadcasted_iota(jnp.int32, (fields, lanes), 1)
    expand = (
        lax.broadcasted_iota(jnp.int32, (lanes, size), 1) // depth
        == lax.broadcasted_iota(jnp.int32, (lanes, size), 0)
    ).astype(f32)
    same_cell = (
        lax.broadcasted_iota(jnp.int32, (depth, size), 1) % depth
        == lax.broadcasted_iota(jnp.int32, (depth, size), 0)
    )

    def swap_rows(value):
        return jnp.where(
            row % 2 == 0, pltpu.roll(value, fields - 1, 0), pltpu.roll(value, 1, 0)
        )

    def swap_lanes(value):
        return jnp.where(
            lane % 2 == 0, pltpu.roll(value, lanes - 1, 1), pltpu.roll(value, 1, 1)
        )

    for slot in range(slots):
        sums = sums_ref[slot]
        across = swap_rows(swap_lanes(sums))
        both = jnp.where((row + lane) % 2 == 0, sums + across, sums - across)
        norm = sums + swap_rows(sums)
        norm = jnp.sum(jnp.where(lane == fields, norm, 0.0), axis=1, keepdims=True)
        both = jnp.where(lane < fields, both / (norm + norm_epsilon), 0.0)
        both = jnp.concatenate([both, jnp.zeros((lanes - fields, lanes), f32)], 0)
        by_out = -jnp.transpose(both)[:fields]
        by_out = jnp.dot(
            by_out, expand, precision=lax.Precision.HIGHEST, preferred_element_type=f32
        )
        high = by_out.astype(bf16).astype(f32)
        low = by_out - high
        for out in range(fields):
            for part, value in enumerate((high, low)):
                spread = jnp.broadcast_to(value[out : out + 1], (depth, size))
                spread = jnp.where(same_cell, spread, 0.0).astype(bf16)
                factor_ref[slot, pl.ds(out * depth, depth), pl.ds(part * size, size)] = spread
    first = lax.broadcasted_iota(jnp.int32, lanes_ref.shape, 0) % lanes
    second = lax.broadcasted_iota(jnp.int32, lanes_ref.shape, 1)
    away = (first - second + lanes) % lanes
    near = (away == 1) | (away == lanes - 1)
    far = (away == 2) | (away == lanes - 2)
    weight = jnp.where(near, near_weight / -far_weight, jnp.where(far, -1.0, 0.0))
    lanes_ref[...] = weight.astype(f32).astype(bf16)


def factors(sums, depth):
    slots, fields, lanes = sums.shape
    size = fields * depth
    return pl.pallas_call(
        functools.partial(factor_kernel, fields, depth),
        out_shape=(
            jax.ShapeDtypeStruct((slots, size, 2 * size), bf16),
            jax.ShapeDtypeStruct((2 * lanes, lanes), bf16),
        ),
        in_specs=[whole()],
        out_specs=(whole(),) * 2,
        compiler_params=params(),
        cost_estimate=NO_COST,
        name="projection_factors",
    )(sums)


def chain_kernel(
    slot, same, scale, last_slot, split, places, named, response_ref, density_refs, scratch
):
    t0_ref, t1_ref, t2_ref, diagonal_ref, sum_ref = scratch
    base, partner_base, kick_at = places
    field_ref = named["field"]
    fields, rows, depth, lanes = field_ref.shape[1:]
    own_row = WIDE
    own_cell = TILE
    zero_shift = named["control"][1]
    factor = named["factor"][0]
    along_lanes = named["lanes"][...]
    size = fields * depth
    block = (fields, depth, lanes)

    def project(pieces):
        raws = [raw for raw, _, _, _ in pieces]
        others = raws if same else [partner for _, partner, _, _ in pieces]
        stacked = jnp.concatenate([other.reshape((size, lanes)) for other in others], 1)
        stacked = jnp.concatenate([stacked, stacked], 0)
        along = jnp.dot(factor, stacked, preferred_element_type=f32)
        results = []
        for index, (raw, _, kick, _) in enumerate(pieces):
            part = along[:, index * lanes : (index + 1) * lanes].reshape(block)
            results.append(kick.astype(f32)[None] * raw.astype(f32) + part)
        for result, (_, _, _, write) in zip(results, pieces):
            write(result)

    partner_own = (lambda row: None) if same else (lambda row: named["partner_field"][0, :, row])
    partner_halo = (
        (lambda name, index: None) if same else (lambda name, index: named["partner_" + name][index])
    )
    depth_cells = pl.ds(own_cell, depth)

    def own(pair, carry):
        def piece(row):
            def write(value):
                t0_ref[:, own_row + row, depth_cells] = value

            return field_ref[0, :, row], partner_own(row), named["perturb"][row], write

        project([piece(2 * pair), piece(2 * pair + 1)])
        return carry

    lax.fori_loop(0, rows // 2, own, 0)

    def outer(row, carry):
        def piece(name, first):
            def write(value):
                t0_ref[:, first + row, depth_cells] = value

            index = (pl.ds(base, fields), row)
            partner = partner_halo(name, (pl.ds(partner_base, fields), row))
            return named[name][index], partner, named["kick_" + name][kick_at, row], write

        project([piece("before", 0), piece("after", own_row + rows)])
        return carry

    lax.fori_loop(0, WIDE, outer, 0)

    pairs = depth // (2 * TILE)
    above_cell = own_cell + depth
    extra = named["below"].shape[0] - 2

    def deep(group, names, firsts, starts):
        def piece(name, first, starts):
            def write(value):
                for line in range(2 * pairs):
                    cells = value[:, line * TILE : (line + 1) * TILE]
                    for start in starts:
                        t0_ref[:, first + 2 * pairs * group + line, start : start + TILE] = cells

            index = (pl.ds(slot * fields, fields), pl.ds(group * pairs, pairs))
            partner = partner_halo(name, index)
            if partner is not None:
                partner = partner.reshape(block)
            kick = named[name][extra, pl.ds(group * pairs, pairs)].reshape((depth, lanes))
            return named[name][index].reshape(block), partner, kick, write

        project([piece(*each) for each in zip(names, firsts, starts)])

    def deep_own(group, carry):
        deep(group, ("below", "above"), (own_row, own_row), ((0,), (above_cell,)))
        return carry

    lax.fori_loop(0, rows // (2 * pairs), deep_own, 0)
    for group in range(INNER // (2 * pairs)):
        both = (0, above_cell)
        firsts = (own_row - INNER, own_row + rows)
        deep(group, ("corner_before", "corner_after"), firsts, (both, both))

    half = TILE // 2
    moved = half
    middle = depth + 2 * half

    def diagonal(value):
        return 0.4 * (value.astype(f32) - 0.5 * centre_weight) - 2.0

    for row in range(rows):
        diagonal_ref[own_row + row, depth_cells] = diagonal(named["local_pot"][row])
    for row in range(INNER):
        diagonal_ref[own_row - INNER + row, depth_cells] = diagonal(
            named["kick_before"][kick_at + 1, WIDE - INNER + row]
        )
        diagonal_ref[own_row + rows + row, depth_cells] = diagonal(
            named["kick_after"][kick_at + 1, row]
        )

    def diagonal_pairs(name, count, first, starts):
        for pair in range(count):
            value = diagonal(named[name][extra + 1, pair])
            for line in range(2):
                for start in starts:
                    diagonal_ref[first + 2 * pair + line, start : start + TILE] = value[
                        line * TILE : (line + 1) * TILE
                    ]

    diagonal_pairs("below", rows // 2, own_row, (0,))
    diagonal_pairs("above", rows // 2, own_row, (above_cell,))
    diagonal_pairs("corner_before", INNER // 2, own_row - INNER, (0, above_cell))
    diagonal_pairs("corner_after", INNER // 2, own_row + rows, (0, above_cell))

    row_index = named["control"][0]
    weights = [named["coefficients"][row_index, order] for order in range(ITERS + 1)]

    if slot == 0:
        sum_ref[...] = jnp.zeros_like(sum_ref)
    else:
        sum_ref[...] = named["density"][...]

    def one_field(f, carry):
        def reader(ref, offset):
            def read(row, start, count):
                first = start + offset
                if first % TILE:
                    first = first + zero_shift
                return ref[row, pl.ds(first, count)]

            return read

        read0 = reader(t0_ref.at[f], 0)
        read1 = reader(t1_ref, moved)
        read2 = reader(t2_ref, moved)
        read_diagonal = reader(diagonal_ref, 0)

        def spans(outer, inner):
            first, last = own_row - outer, own_row + rows + outer
            narrow, wide = (own_cell, depth), (own_cell - half, middle)
            inner_first, inner_last = own_row - inner, own_row + rows + inner
            groups = [(list(range(first, inner_first)), narrow)]
            for row in range(inner_first, inner_last, GROUP):
                groups.append((list(range(row, min(row + GROUP, inner_last))), wide))
            groups.append((list(range(inner_last, last)), narrow))
            return [(lines, span) for lines, span in groups if lines]

        def sweep(read, groups, finish):
            window, window_span = {}, None
            for lines, span in groups:
                if span != window_span:
                    window, window_span = {}, span
                start, count = span
                for row in range(lines[0] - REACH, lines[-1] + REACH + 1):
                    if row not in window:
                        window[row] = read(row, start, count)
                centres = jnp.concatenate([window[row] for row in lines], 0)
                high = centres.astype(bf16)
                low = (centres - high.astype(f32)).astype(bf16)
                sides = jnp.dot(
                    jnp.concatenate([high, low], 1), along_lanes, preferred_element_type=f32
                )
                results = []
                for index, row in enumerate(lines):
                    centre = window[row]
                    near = window[row - 1] + window[row + 1]
                    far = window[row - 2] + window[row + 2]
                    near = near + (read(row, start - 1, count) + read(row, start + 1, count))
                    far = far + (read(row, start - 2, count) + read(row, start + 2, count))
                    side = sides[index * count : (index + 1) * count]
                    value = read_diagonal(row, start, count) * centre
                    value = value - far_scale * (side + ((near_weight / -far_weight) * near - far))
                    results.append(finish(row, start, count, centre, value))
                for row, (store, result) in zip(lines, results):
                    store(row, result)
                for row in [row for row in window if row < lines[-1] + 1 - REACH]:
                    del window[row]

        def store_to(ref, start, count):
            def store(row, value):
                ref[row, pl.ds(start + moved, count)] = value

            return store

        def first_result(row, start, count, centre, value):
            return store_to(t1_ref, start, count), 0.5 * value

        def second_result(row, start, count, centre, value):
            return store_to(t2_ref, start, count), value - read0(row, start, count)

        def last_result(row, start, count, centre, value):
            first = read1(row, start, count)
            answer = weights[0] * read0(row, start, count) + weights[1] * first
            answer = answer + (weights[2] * centre + weights[3] * (value - first))
            answer = answer.astype(bf16)
            line = row - own_row
            added = sum_ref[line] + answer.astype(f32) * field_ref[0, f, line].astype(f32)

            def store(row, pair):
                response_ref[0, f, line] = pair[0]
                sum_ref[line] = pair[1]

            return store, (answer, added)

        sweep(read0, spans(INNER, INNER - REACH), first_result)
        sweep(read1, spans(REACH, 0), second_result)
        lines = range(own_row, own_row + rows)
        narrow = (own_cell, depth)
        groups = [(list(lines[at : at + GROUP]), narrow) for at in range(0, rows, GROUP)]
        sweep(read2, groups, last_result)
        return carry

    lax.fori_loop(0, fields, one_field, 0)

    if not last_slot:
        density_refs[0][...] = sum_ref[...]
        return
    total = sum_ref[...] * scale
    if not split:
        density_refs[0][...] = total
        return
    turned = pltpu.roll(total, lanes // 2, 2)
    total = jnp.where(named["control"][2] == 0, total, turned)
    density_refs[0][...] = total
    upper, lower = total[:, : depth // 2], total[:, depth // 2 :]
    lane = lax.broadcasted_iota(jnp.int32, upper.shape, 2)
    density_refs[1][...] = jnp.where(lane < lanes // 2, pltpu.roll(upper, lanes // 2, 2), lower)


DEEP_NAMES = ("below", "above", "corner_before", "corner_after")


def chain(slot, orbitals, partner, halos, partner_halos, perturb, local_pot, coefficients, control,
          matrices, scale, split, carried):
    slots, fields, rows, depth, lanes = orbitals.shape
    same = partner is None
    names, operands, specs = [], [], []
    last_slot = slot == slots - 1

    def add(name, value, spec):
        names.append(name)
        operands.append(value)
        specs.append(spec)

    block = (1, fields, rows, depth, lanes)
    at_slot = pl.BlockSpec(block, lambda step: (slot, 0, 0, 0, 0))

    def add_halos(prefix, halos):
        for name, value in zip(("before", "after"), halos[0][slot]):
            add(prefix + name, value, whole())
        for name, value in zip(DEEP_NAMES, halos[1]):
            add(prefix + name, value, whole())

    add("field", orbitals, at_slot)
    add_halos("", halos)
    kick_shared = halos[2][0] is halos[0][slot][0]
    if not kick_shared:
        for name, value in zip(("before", "after"), halos[2]):
            add("kick_" + name, value, whole())
    if not same:
        add("partner_field", partner, at_slot)
        add_halos("partner_", partner_halos)
    places = (halos[0][slot][2], None if same else partner_halos[0][slot][2], halos[2][2])
    add("perturb", perturb, whole())
    add("local_pot", local_pot, whole())
    add("coefficients", coefficients, in_smem())
    add("control", control, in_smem())
    add("factor", matrices[0], pl.BlockSpec((1,) + matrices[0].shape[1:], lambda step: (slot, 0, 0)))
    add("lanes", matrices[1], whole())
    aliases = {}
    if slot:
        add("density", carried[1], whole())
        aliases = {len(names): 0}
        add("response", carried[0], pl.BlockSpec(memory_space=pl.ANY))

    density_shapes = [jax.ShapeDtypeStruct((rows, depth, lanes), f32)]
    if last_slot and split:
        density_shapes.append(jax.ShapeDtypeStruct((rows, depth // 2, lanes), f32))

    def kernel(*refs):
        named = dict(zip(names, refs))
        if kick_shared:
            named["kick_before"] = named["before"]
            named["kick_after"] = named["after"]
        outs = refs[len(names) : len(names) + 1 + len(density_shapes)]
        scratch = refs[len(names) + len(outs) :]
        chain_kernel(
            slot, same, scale, last_slot, split, places, named, outs[0], outs[1:], scratch
        )

    long_rows = rows + 2 * WIDE
    long_depth = depth + 2 * TILE
    return pl.pallas_call(
        kernel,
        grid=(1,),
        out_shape=(jax.ShapeDtypeStruct(orbitals.shape, bf16), *density_shapes),
        in_specs=specs,
        out_specs=(at_slot,) + (whole(),) * len(density_shapes),
        scratch_shapes=[
            pltpu.VMEM((fields, long_rows, long_depth, lanes), f32),
            pltpu.VMEM((long_rows, long_depth + TILE, lanes), f32),
            pltpu.VMEM((long_rows, long_depth + TILE, lanes), f32),
            pltpu.VMEM((long_rows, long_depth, lanes), f32),
            pltpu.VMEM((rows, depth, lanes), f32),
        ],
        input_output_aliases=aliases,
        compiler_params=params(),
        cost_estimate=NO_COST,
        name="response_chain",
    )(*operands)


def from_behind(value, axis, steps):
    count = lax.axis_size(axis)
    pairs = [(source, (source + steps) % count) for source in range(count)]
    return lax.ppermute(value, axis, pairs)


def route(blocks, shift_count):
    groups = lax.axis_size("ka")
    if groups == 2:
        return from_behind(blocks, "ka", -1)
    moved = blocks
    for bit_index in range((groups - 1).bit_length()):
        shifted = from_behind(moved, "ka", -(1 << bit_index))
        taken = shift_count >> bit_index & 1 == 1
        moved = jnp.where(taken, shifted, moved)
    return moved


def finish_kernel(total_ref, other_ref, out_ref):
    total = total_ref[...]
    other = other_ref[...]
    lanes = total.shape[2]
    depth = total.shape[1]
    kept = lanes // 2
    out_ref[:, : depth // 2] = (total[:, : depth // 2] + other)[:, :, :kept]
    out_ref[:, depth // 2 :] = (total[:, depth // 2 :] + pltpu.roll(other, kept, 2))[:, :, :kept]


def finish(total, packed):
    other = from_behind(packed, "ka", 1)
    rows, depth, lanes = total.shape
    return pl.pallas_call(
        finish_kernel,
        out_shape=jax.ShapeDtypeStruct((rows, depth, lanes // 2), f32),
        in_specs=[whole(), whole()],
        out_specs=whole(),
        compiler_params=params(),
        cost_estimate=NO_COST,
        name="density_sum",
    )(total, other)


def body(orbitals, coefficients, local_pot, perturb, q_index):
    groups = lax.axis_size("ka")
    shift_count = q_index[0] % groups
    group_index = lax.axis_index("ka")
    slots, bands, parts, rows, depth, lanes = orbitals.shape
    fields = orbitals.reshape((slots, bands * parts, rows, depth, lanes))
    partner_group = (group_index + shift_count) % groups
    scale = 2.0 / (slots * groups)
    split = groups == 2

    def work(shifted):
        halos = exchange(fields, (perturb, local_pot), not shifted)
        partner, partner_halos = None, None
        if shifted:
            partner = route(fields, shift_count)
            partner_halos = exchange(partner, (), True, halos[0][0][:2] + halos[1][2:])
        last_halos = partner_halos if shifted else halos
        after = from_behind(last_halos[3], "ka", 1)
        sums = inner_products(fields, perturb, partner, after)
        send_rows(partner if shifted else fields, last_halos, (sums,))
        matrices = factors(sums, depth)
        carried = None
        for slot in range(slots):
            row_index = partner_group * slots + slot
            control = jnp.stack([row_index, jnp.zeros_like(row_index), group_index])
            carried = chain(
                slot, fields, partner, halos, partner_halos, perturb, local_pot, coefficients,
                control.astype(jnp.int32), matrices, scale, split, carried,
            )
        if split:
            return carried[0], finish(carried[1], carried[2])
        return carried[0], lax.psum_scatter(carried[1], "ka", scatter_dimension=2, tiled=True)

    responses, density = lax.cond(shift_count == 0, lambda: work(False), lambda: work(True))
    return responses.reshape(orbitals.shape), density


def solution(mesh):
    return jax.shard_map(
        body,
        mesh=mesh,
        in_specs=(
            P("ka", None, None, "sy", "sz", None),
            P(),
            P("sy", "sz", None),
            P("sy", "sz", None),
            P(),
        ),
        out_specs=(P("ka", None, None, "sy", "sz", None), P("sy", "sz", "ka")),
        check_vma=False,
    )
```
